256 devices in a mesh: dp: 32 (over x, z_hi, core), shard: 8 (over y, z_lo).
Axes of the slice: x: 4, y: 4, z: 8 (z_hi: 4, z_lo: 2; z = z_hi * 2 + z_lo), core: 2. Of those that a mesh axis runs over, the one named last changes fastest.
Arguments:
- residual_input: bfloat16 [768, 6144], P('dp'), may hold values from -6 to 6
- attention_mixture: bfloat16 [768, 6144], P('dp', 'shard'), may hold values from -6 to 6
- output_gradient: bfloat16 [768, 6144], P('dp'), may hold values from -6 to 6
- norm_gain_vector: float32 [6144], replicated, may hold values from 0.25 to 1.75
- routes: int32 [768, 2], P('dp'), may hold values from 0 to 7, all different within a row; in each aligned block of 24 rows (0 to 23, 24 to 47, ...) at most 12 rows name the same one
- router_weight: float32 [768, 2], P('dp'), may hold values from 0.2 to 1
- gate_weight: bfloat16 [8, 6144, 8192], P('shard', None, 'dp'), may hold values from -0.078125 to 0.078125
- up_weight: bfloat16 [8, 6144, 8192], P('shard', None, 'dp'), may hold values from -0.078125 to 0.078125
- down_weight: bfloat16 [8, 8192, 6144], P('shard', 'dp'), may hold values from -0.0625 to 0.0625
- gate_adapter_first: bfloat16 [8, 6144, 16], P('shard'), may hold values from -0.078125 to 0.078125
- gate_adapter_second: bfloat16 [8, 16, 8192], P('shard', None, 'dp'), may hold values from -1.5 to 1.5
- attention_adapter_first: bfloat16 [6144, 16], P('shard'), may hold values from -0.078125 to 0.078125
- attention_adapter_second: bfloat16 [16, 6144], P(None, 'shard'), may hold values from -1.5 to 1.5
Outputs:
- residual_gradient: bfloat16 [768, 6144], P('dp', 'shard')
- gate_first_gradient: float32 [8, 6144, 16], P('shard')
- gate_second_gradient: float32 [8, 16, 8192], P('shard', None, 'dp')
- attention_first_gradient: float32 [6144, 16], P('shard')
- attention_second_gradient: float32 [16, 6144], P(None, 'shard')
The draws below stay inside these ranges and needn't reach their ends.
Inputs may be any that keep to these rules, and one draw needn't show every extreme that they name: No expert is named by more than 12 routes of one aligned block of 24 tokens.
All inputs are finite; a program needn't handle non-finite values.
Results may differ from the reference program's by a relative error of at most 0.023.
Values may be sent and summed in bfloat16 or wider, within the bound.
A program may use at most 128 MiB of HBM per device.

```python
import math
import jax
import jax.numpy as jnp
import numpy as np
from jax import lax

MODEL_WIDTH = 6144
EXPERT_COUNT = 8
HIDDEN_UNITS = 8192
ADAPTER_RANK = 16
TOK_DP = 24
TOKENS = 768
CAP = 12


def shard_levels(own_key, shape, shards, least, high):
    def one(dim, blocks):
        heights = jax.random.uniform(jax.random.fold_in(jax.random.fold_in(own_key, 6), dim), (blocks,), jnp.float32, least / len(shards), high / len(shards))
        return jnp.repeat(jnp.exp(heights), shape[dim] // blocks).reshape((-1,) + (1,) * (len(shape) - dim - 1))

    level = one(*shards[0])
    for cut in shards[1:]:
        level = level * one(*cut)
    return level


def shared_out(key, own, number, rows, number_of, top, reach, slope):
    ranking = jax.random.permutation(key, number_of)
    heavy_load, usual = shares(number_of, rows * top, reach, slope, True), shares(number_of, rows * top, reach, slope, False)
    places = jnp.arange(number_of)

    def named(tallies, offset_by):
        used = int((tallies > 0).sum())
        fixed = max(1, used // 4)
        passed = fixed + (places - fixed + offset_by * (used - fixed)) % max(1, number_of - fixed)
        return jnp.zeros((number_of,), jnp.int32).at[ranking[jnp.where(places < fixed, places, passed)]].set(jnp.asarray(tallies, jnp.int32))

    tallies = jnp.where(number % 4 == 0, named(heavy_load, number // 4), named(usual, number - number // 4 - 1))
    mixed = jax.random.permutation(jax.random.fold_in(own, 3), number_of)
    donor, sink = mixed[0:number_of // 2 * 2:2], mixed[1:number_of // 2 * 2:2]
    room = jnp.minimum(tallies[donor] - 1, reach - tallies[sink]) // 2
    room = jnp.where((donor == ranking[0]) | (sink == ranking[0]) | (tallies[sink] == 0), 0, jnp.maximum(room, 0))
    passed = jax.random.randint(jax.random.fold_in(own, 4), (number_of // 2,), 0, 1 << 20) % (room + 1)
    tallies = tallies.at[donor].add(-passed).at[sink].add(passed)
    items = jnp.searchsorted(jnp.cumsum(tallies), jnp.arange(rows * top), side="right").astype(jnp.int32)
    grid = items.reshape(top, rows).T
    grid = grid[jax.random.permutation(jax.random.fold_in(own, 1), rows)]
    offset_by = jax.random.randint(jax.random.fold_in(own, 2), (rows, 1), 0, top)
    return jnp.take_along_axis(grid, (jnp.arange(top)[None, :] + offset_by) % top, axis=1)


def shares(amount, total, bound, lean, full):
    portions = [(1 << 20) // math.isqrt(grade ** lean) + 1 for grade in range(1, amount + 1)]
    largest = bound if full else min(bound, max(-(-total // amount), total * portions[0] // sum(portions)))
    least = 1 if total - largest >= amount - 1 else 0
    counts, surplus = [largest] + [least] * (amount - 1), total - largest - least * (amount - 1)
    while surplus > 0:
        free = [i for i in range(1, amount) if counts[i] < largest] or [i for i in range(1, amount) if counts[i] < bound]
        whole, left = sum([portions[i] for i in free]), surplus
        for i in free:
            addition = min(bound - counts[i], max(1, left * portions[i] // whole), surplus)
            counts[i] = counts[i] + addition
            surplus = surplus - addition
    return np.array(counts)


def normal_values(stream_key, extent, deviation, reach, cuts=(), held_as=jnp.bfloat16):
    level = shard_levels(stream_key, extent, cuts, -0.22, 0.18) if cuts else 1.0
    result = jax.random.normal(stream_key, extent, jnp.float32) * deviation * level
    return jnp.minimum(jnp.maximum(result, -reach), reach).astype(held_as)


def setup_inputs(seed: int = 0) -> dict:
    keys = jax.random.split(jax.random.key(seed), 14)
    residual_input = normal_values(keys[0], (TOKENS, MODEL_WIDTH), 1.0, 6.0, ((0, 32),))
    attention_mixture = normal_values(keys[1], (TOKENS, MODEL_WIDTH), 1.0, 6.0, ((0, 32), (1, 8)))
    output_gradient = normal_values(keys[2], (TOKENS, MODEL_WIDTH), 1.0, 6.0, ((0, 32),))
    norm_gain_vector = jnp.clip(1.0 + 0.15 * jax.random.normal(keys[3], (MODEL_WIDTH,), jnp.float32), 0.25, 1.75)
    routes_keys = jax.random.split(jax.random.fold_in(keys[4], 1), TOKENS // TOK_DP)
    routes_turns = jax.random.permutation(jax.random.fold_in(keys[4], 3), TOKENS // TOK_DP)
    routes = jax.vmap(lambda own, number: shared_out(jax.random.fold_in(keys[4], 2), own, number, TOK_DP, EXPERT_COUNT, 2, CAP, 2))(routes_keys, routes_turns).reshape((TOKENS, 2))
    router_weight = jnp.clip(0.2 + 0.8 * jax.random.uniform(keys[5], (TOKENS, 2), jnp.float32) ** shard_levels(keys[5], (TOKENS, 2), ((0, 32),), -0.2, 0.2), 0.2, 1.0)
    gate_weight = normal_values(keys[6], (EXPERT_COUNT, MODEL_WIDTH, HIDDEN_UNITS), MODEL_WIDTH ** -0.5, 0.078125, ((0, 8), (2, 32)))
    up_weight = normal_values(keys[7], (EXPERT_COUNT, MODEL_WIDTH, HIDDEN_UNITS), MODEL_WIDTH ** -0.5, 0.078125, ((0, 8), (2, 32)))
    down_weight = normal_values(keys[8], (EXPERT_COUNT, HIDDEN_UNITS, MODEL_WIDTH), HIDDEN_UNITS ** -0.5, 0.0625, ((0, 8), (1, 32)))
    gate_adapter_first = normal_values(keys[9], (EXPERT_COUNT, MODEL_WIDTH, ADAPTER_RANK), MODEL_WIDTH ** -0.5, 0.078125, ((0, 8),))
    gate_adapter_second = normal_values(keys[10], (EXPERT_COUNT, ADAPTER_RANK, HIDDEN_UNITS), ADAPTER_RANK ** -0.5, 1.5, ((0, 8), (2, 32)))
    attention_adapter_first = normal_values(keys[11], (MODEL_WIDTH, ADAPTER_RANK), MODEL_WIDTH ** -0.5, 0.078125, ((0, 8),))
    attention_adapter_second = normal_values(keys[12], (ADAPTER_RANK, MODEL_WIDTH), ADAPTER_RANK ** -0.5, 1.5, ((1, 8),))
    return {"residual_input": residual_input, "attention_mixture": attention_mixture, "output_gradient": output_gradient, "norm_gain_vector": norm_gain_vector, "routes": routes, "router_weight": router_weight, "gate_weight": gate_weight, "up_weight": up_weight, "down_weight": down_weight, "gate_adapter_first": gate_adapter_first, "gate_adapter_second": gate_adapter_second, "attention_adapter_first": attention_adapter_first, "attention_adapter_second": attention_adapter_second}


EPSILON = 1e-05
ADAPTER_SCALE = 0.5

def norm_rows(hidden, gain):
    wide = hidden.astype(jnp.float32)
    radius = lax.rsqrt(lax.optimization_barrier(jnp.mean(wide * wide, axis=1)) + EPSILON)
    return (radius, (wide * radius[:, None] * gain).astype(jnp.bfloat16))

def slot_table(route_block, expert_ids, capacity):
    flat = route_block.reshape(-1)
    count = flat.shape[0]
    same = (flat[:, None] == flat[None, :]).astype(jnp.int32)
    earlier = (jnp.arange(count, dtype=jnp.int32)[:, None] > jnp.arange(count, dtype=jnp.int32)[None, :]).astype(jnp.int32)
    slot = lax.optimization_barrier(jnp.sum(same * earlier, axis=1))
    match = (flat[None, None, :] == expert_ids[:, None, None]) & (slot[None, None, :] == jnp.arange(capacity, dtype=jnp.int32)[None, :, None])
    return match.astype(jnp.float32).reshape(expert_ids.shape[0], capacity, count // 2, 2)

def expert_layer_backward(inputs):
    input_rows, rows_dy, gate_matrix, up_w, down_w, adapt_a, adapter_second = inputs
    lowrank_product = jnp.dot(input_rows, adapt_a, preferred_element_type=jnp.float32).astype(jnp.bfloat16)
    gate_values = jnp.dot(input_rows, gate_matrix, preferred_element_type=jnp.float32) + ADAPTER_SCALE * jnp.dot(lowrank_product, adapter_second, preferred_element_type=jnp.float32)
    upper = jnp.dot(input_rows, up_w, preferred_element_type=jnp.float32)
    dact = jnp.dot(rows_dy, down_w.T, preferred_element_type=jnp.float32)
    sigm = jax.nn.sigmoid(gate_values)
    gate_cotangent = (dact * upper * sigm * (1.0 + gate_values * (1.0 - sigm))).astype(jnp.bfloat16)
    dup = (dact * gate_values * sigm).astype(jnp.bfloat16)
    backward_result = ADAPTER_SCALE * jnp.dot(gate_cotangent, adapter_second.T, preferred_element_type=jnp.float32)
    grad_a = jnp.dot(input_rows.astype(jnp.float32).T, backward_result, precision=lax.Precision.HIGHEST)
    second_factor_gradient = ADAPTER_SCALE * jnp.dot(lowrank_product.T, gate_cotangent, preferred_element_type=jnp.float32)
    row_gradient = jnp.dot(gate_cotangent, gate_matrix.T, preferred_element_type=jnp.float32) + jnp.dot(dup, up_w.T, preferred_element_type=jnp.float32)
    row_gradient = row_gradient + jnp.dot(backward_result, adapt_a.astype(jnp.float32).T, precision=lax.Precision.HIGHEST)
    return (row_gradient, grad_a, second_factor_gradient)

def reference(residual_input, attention_mixture, output_gradient, norm_gain_vector, routes, router_weight, gate_weight, up_weight, down_weight, gate_adapter_first, gate_adapter_second, attention_adapter_first, attention_adapter_second):
    blocks = TOKENS // TOK_DP
    radius, normed = norm_rows(residual_input, norm_gain_vector)
    expert_ids = jnp.arange(EXPERT_COUNT, dtype=jnp.int32)
    match = jax.vmap(lambda block: slot_table(block, expert_ids, CAP))(routes.reshape(blocks, TOK_DP, 2))
    chooser = lax.optimization_barrier(jnp.sum(match, axis=4))
    weighted = lax.optimization_barrier(jnp.sum(match * router_weight.reshape(blocks, 1, 1, TOK_DP, 2), axis=4))
    packed_input_rows = jnp.einsum('becT,bTd->ebcd', chooser, normed.astype(jnp.float32).reshape(blocks, TOK_DP, MODEL_WIDTH), precision=lax.Precision.HIGHEST)
    packed_input_rows = packed_input_rows.astype(jnp.bfloat16).reshape(EXPERT_COUNT, blocks * CAP, MODEL_WIDTH)
    packed_output_gradient = jnp.einsum('becT,bTd->ebcd', weighted, output_gradient.astype(jnp.float32).reshape(blocks, TOK_DP, MODEL_WIDTH), precision=lax.Precision.HIGHEST)
    packed_output_gradient = packed_output_gradient.astype(jnp.bfloat16).reshape(EXPERT_COUNT, blocks * CAP, MODEL_WIDTH)
    row_gradient, gate_first_gradient, gate_second_gradient = lax.map(expert_layer_backward, (packed_input_rows, packed_output_gradient, gate_weight, up_weight, down_weight, gate_adapter_first, gate_adapter_second))
    grad_norm_in = jnp.einsum('becT,ebcd->bTd', chooser, row_gradient.reshape(EXPERT_COUNT, blocks, CAP, MODEL_WIDTH), precision=lax.Precision.HIGHEST).reshape(TOKENS, MODEL_WIDTH)
    wide = residual_input.astype(jnp.float32)
    spread = norm_gain_vector * grad_norm_in
    stat = lax.optimization_barrier(jnp.mean(spread * wide, axis=1))
    residual_gradient = (output_gradient.astype(jnp.float32) + radius[:, None] * spread - wide * (radius ** 3 * stat)[:, None]).astype(jnp.bfloat16)
    mixture_lowrank = jnp.dot(attention_mixture, attention_adapter_first, preferred_element_type=jnp.float32).astype(jnp.bfloat16)
    backward_lowrank = jnp.dot(residual_gradient, attention_adapter_second.T, preferred_element_type=jnp.float32).astype(jnp.bfloat16)
    attention_first_gradient = ADAPTER_SCALE * jnp.dot(attention_mixture.T, backward_lowrank, preferred_element_type=jnp.float32)
    attention_second_gradient = ADAPTER_SCALE * jnp.dot(mixture_lowrank.T, residual_gradient, preferred_element_type=jnp.float32)
    return (residual_gradient, gate_first_gradient, gate_second_gradient, attention_first_gradient, attention_second_gradient)
```

```python
import functools

import jax
import jax.numpy as jnp
from jax import lax
from jax.experimental import pallas as pl
from jax.experimental.pallas import tpu as pltpu
from jax.sharding import PartitionSpec as P

CAP = 12
EPSILON = 1e-05
SCALE = 0.5
NX = 4
F32 = jnp.float32
BF16 = jnp.bfloat16
MESH = pl.DeviceIdType.MESH
NN = (((1,), (0,)), ((), ()))
NT = (((1,), (1,)), ((), ()))


def mm(a, b, dims=NN):
    return lax.dot_general(a, b, dims, preferred_element_type=F32)


def two_parts(value):
    high = value.astype(BF16)
    return high, (value - high.astype(F32)).astype(BF16)


def column(row, count):
    eye = lax.broadcasted_iota(jnp.int32, (count, count), 0) == lax.broadcasted_iota(
        jnp.int32, (count, count), 1
    )
    return jnp.sum(jnp.where(eye, jnp.broadcast_to(row, (count, count)), 0.0), axis=1, keepdims=True)


def row_of(col, count):
    eye = lax.broadcasted_iota(jnp.int32, (count, count), 0) == lax.broadcasted_iota(
        jnp.int32, (count, count), 1
    )
    return jnp.sum(jnp.where(eye, jnp.broadcast_to(col, (count, count)), 0.0), axis=0, keepdims=True)


def kernel(
    nz,
    ns,
    kc,
    hid_ref,
    mix_ref,
    og_ref,
    gain_ref,
    routes_ref,
    rw_ref,
    wg_hbm,
    wu_hbm,
    wd_hbm,
    a1_hbm,
    a2_ref,
    att1_ref,
    att2_ref,
    rg_ref,
    ga_ref,
    gs_ref,
    af_ref,
    as_ref,
    wg,
    wu,
    wd,
    a1,
    rb,
    sb0,
    G,
    acc_g,
    acc_u,
    acc_d,
    acc_l,
    dg,
    du,
    bk,
    TB,
    TR,
    SB,
    XR1,
    XR2,
    ZB,
    ZR,
    EB,
    E,
    PB,
    PR,
    A,
    AR,
    F,
    rad_ref,
    w_sem,
    p0_s,
    p0_r,
    z_s,
    z_r,
    x_s,
    x_r,
    c_s,
    c_r,
    t_s,
    t_r,
    x1_s,
    x1_r,
    x2_s,
    x2_r,
    zz_s,
    zz_r,
    e_s,
    e_r,
    e_l,
    q_s,
    q_r,
    a_s,
    a_r,
    f_s,
    f_r,
):
    nch = ns // 2
    nd = NX * nz * 2
    chips = NX * nz
    toks = hid_ref.shape[0]
    width = hid_ref.shape[1]
    hw = width // 2
    frame = chips * 32
    rows = chips * 24
    lanes = kc // 128
    d = lax.axis_index("dp")
    s = lax.axis_index("shard")
    core = lax.rem(d, 2)
    zh = lax.rem(d // 2, nz)
    xx = d // (2 * nz)
    q = xx * nz + zh
    other = 1 - core

    def dp_of(x_, z_, c_):
        return (x_ * nz + z_) * 2 + c_

    xp, xm, x2 = lax.rem(xx + 1, NX), lax.rem(xx + 3, NX), lax.rem(xx + 2, NX)
    dev_c = (dp_of(xx, zh, other), s)
    dev_xp = (dp_of(xp, zh, core), s)
    dev_xm = (dp_of(xm, zh, core), s)

    def zpeer(o):
        return lax.rem(zh + o, nz)

    def dev_z(o):
        return (dp_of(xx, zpeer(o), core), s)

    def rcopy(src, dst, ssem, rsem, dev):
        return pltpu.make_async_remote_copy(
            src_ref=src, dst_ref=dst, send_sem=ssem, recv_sem=rsem, device_id=dev, device_id_type=MESH
        )

    w_copies = [
        pltpu.make_async_copy(a1_hbm, a1, w_sem.at[0]),
        pltpu.make_async_copy(wg_hbm, wg, w_sem.at[1]),
        pltpu.make_async_copy(wu_hbm, wu, w_sem.at[2]),
    ] + [
        pltpu.make_async_copy(wd_hbm.at[:, pl.ds(i * kc, kc)], wd.at[i], w_sem.at[3 + i])
        for i in range(2 * nch)
    ]
    for copy in w_copies:
        copy.start()

    barrier = pltpu.get_barrier_semaphore()

    def greet_dp(o, carry):
        pl.semaphore_signal(barrier, inc=1, device_id=(lax.rem(d + o, nd), s), device_id_type=MESH)
        return carry

    lax.fori_loop(1, nd, greet_dp, 0)

    def greet_shard(o, carry):
        there = lax.rem(s + o, ns)
        pl.semaphore_signal(barrier, inc=1, device_id=(d, there), device_id_type=MESH)
        pl.semaphore_signal(barrier, inc=1, device_id=(dp_of(xx, zh, other), there), device_id_type=MESH)
        return carry

    lax.fori_loop(1, ns, greet_shard, 0)

    hid = hid_ref[...].astype(F32)
    radius = lax.rsqrt(jnp.mean(hid * hid, axis=1, keepdims=True) + EPSILON)
    rad_ref[...] = jnp.broadcast_to(radius, rad_ref.shape)
    normed = hid * radius * gain_ref[...]
    tok = jnp.concatenate([normed, og_ref[...].astype(F32)], axis=0).astype(BF16)

    r0 = column(routes_ref[0:1, :].astype(F32), toks)
    r1 = column(routes_ref[1:2, :].astype(F32), toks)
    w0 = column(rw_ref[0:1, :], toks)
    w1 = column(rw_ref[1:2, :], toks)
    lane = lax.broadcasted_iota(jnp.int32, (toks, 128), 1)
    lower = (
        lax.broadcasted_iota(jnp.int32, (toks, toks), 0) > lax.broadcasted_iota(jnp.int32, (toks, toks), 1)
    ).astype(F32).astype(BF16)
    lane_e = (lane // 16).astype(F32)
    named_all = jnp.where((r0 == lane_e) | (r1 == lane_e), 1.0, 0.0)
    slot_all = mm(lower, named_all.astype(BF16))
    place_f = lax.rem(lane, 16).astype(F32)
    choose_all = jnp.where(slot_all + (4 * core).astype(F32) == place_f, named_all, 0.0).astype(BF16)
    mine = jnp.broadcast_to(s.astype(F32), (toks, 128))
    hit0 = jnp.where(r0 == mine, 1.0, 0.0)
    hit1 = jnp.where(r1 == mine, 1.0, 0.0)
    named = hit0 + hit1
    weight = hit0 * w0 + hit1 * w1
    slot = mm(lower, named.astype(BF16)) + (CAP * core).astype(F32)
    row_x = jnp.where(lane < 24, lane, -1).astype(F32)
    row_y = jnp.where(
        (lane >= 24) & (lane < 32), lane - 8, jnp.where((lane >= 32) & (lane < 48), lane - 32, -1)
    ).astype(F32)
    hot_x = jnp.where(slot == row_x, named, 0.0)
    hot_y = jnp.where(slot == row_y, named, 0.0)
    blank = jnp.zeros((128 - 2 * toks, 128), F32)
    hot = jnp.concatenate([hot_x, hot_y, blank], axis=0).T
    scale = jnp.concatenate([hot_x, hot_y * weight, blank], axis=0).T
    hot = hot[0:48, 0:48].astype(BF16)
    scale = jnp.sum(scale[0:48, :], axis=1, keepdims=True)
    for j in range(2 * nch):
        part = mm(hot, tok[:, j * kc : (j + 1) * kc]) * scale
        sb0[j] = part.astype(BF16)

    pl.semaphore_wait(barrier, nd - 1 + 2 * (ns - 1))

    swap = rcopy(sb0.at[pl.ds(other * nch, nch)], rb, p0_s, p0_r, dev_c)
    swap.start()

    PB[40:64, 0:16] = mm(mix_ref[...], att1_ref[...], NT)

    acc_g[...] = jnp.zeros_like(acc_g)
    acc_u[...] = jnp.zeros_like(acc_u)
    acc_d[...] = jnp.zeros_like(acc_d)
    acc_l[...] = jnp.zeros_like(acc_l)

    swap.wait_recv()

    def z_copy(k, o):
        ref = G.at[core * nch + k, q]
        return rcopy(ref, ref, z_s.at[k, o - 1], z_r.at[k, o - 1], dev_z(o))

    def z_start(k, carry):
        G[core * nch + k, q] = (sb0[core * nch + k].astype(F32) + rb[k].astype(F32)).astype(BF16)
        for o in range(1, nz):
            z_copy(k, o).start()
        return carry

    lax.fori_loop(0, nch, z_start, 0)

    def x_copy(k, which):
        ch = core * nch + k
        half = nz // 2
        if which == 0:
            ref, dev = G.at[ch, pl.ds(xx * nz, nz)], dev_xp
        elif which == 1:
            ref, dev = G.at[ch, pl.ds(xx * nz, nz)], dev_xm
        elif which == 2:
            ref, dev = G.at[ch, pl.ds(xm * nz, half)], dev_xp
        else:
            ref, dev = G.at[ch, pl.ds(xp * nz + half, half)], dev_xm
        return rcopy(ref, ref, x_s.at[k, which], x_r.at[k, which], dev)

    def c_copy(k):
        ref = G.at[core * nch + k]
        return rcopy(ref, ref, c_s.at[k], c_r.at[k], dev_c)

    def product(ch):
        xrows = G[ch, :, 0:32, :].reshape(frame, kc)
        yrows = G[ch, :, 16:48, :].reshape(frame, kc)
        at = pl.ds(pl.multiple_of(ch * kc, kc), kc)
        acc_g[...] += mm(xrows, wg[at, :])
        acc_u[...] += mm(xrows, wu[at, :])
        acc_l[:, 0:16] += mm(xrows, a1[ch], NT)
        acc_d[...] += mm(yrows, wd[ch], NT)

    def gather_step(i, carry):
        @pl.when(i < nch)
        def _():
            for o in range(1, nz):
                z_copy(i, o).wait_recv()
            x_copy(i, 0).start()
            x_copy(i, 1).start()

        @pl.when((i >= 1) & (i < nch + 1))
        def _():
            k = i - 1
            x_copy(k, 0).wait_recv()
            x_copy(k, 2).start()
            x_copy(k, 1).wait_recv()
            x_copy(k, 3).start()

        @pl.when(i == 2)
        def _():
            for copy in w_copies:
                copy.wait()

        @pl.when((i >= 2) & (i < nch + 2))
        def _():
            k = i - 2
            x_copy(k, 2).wait_recv()
            x_copy(k, 3).wait_recv()
            c_copy(k).start()
            product(core * nch + k)

        @pl.when(i >= 3)
        def _():
            k = i - 3
            c_copy(k).wait_recv()
            product(other * nch + k)

        return carry

    lax.fori_loop(0, nch + 3, gather_step, 0)

    low = acc_l[...].astype(BF16)
    gate = acc_g[...] + SCALE * mm(low[:, 0:16], a2_ref[...])
    hidden = gate.shape[1]
    gate = gate.reshape(chips, 32, hidden)[:, 0:24, :]
    upper = acc_u[...].reshape(chips, 32, hidden)[:, 0:24, :]
    dact = acc_d[...].reshape(chips, 32, hidden)
    dact = jnp.concatenate([dact[:, 16:32, :], dact[:, 8:16, :]], axis=1)
    sig = 1.0 / (1.0 + jnp.exp(-gate))
    dgate = dact * upper * sig * (1.0 + gate * (1.0 - sig))
    dup = dact * gate * sig
    du[...] = dup.reshape(rows, hidden).astype(BF16)
    dgate_rows = dgate.reshape(rows, hidden).astype(BF16)
    dg[...] = dgate_rows
    bk[...] = (SCALE * mm(dgate_rows, a2_ref[...], NT)).astype(BF16)
    dgate_frame = (
        jnp.concatenate([dgate, jnp.zeros((chips, 8, hidden), F32)], axis=1)
        .reshape(frame, hidden)
        .astype(BF16)
    )
    low_t = acc_l[...].T[0:16, :].astype(BF16)
    gs_ref[...] = SCALE * mm(low_t, dgate_frame)
    back_t = SCALE * mm(a2_ref[...], dgate_frame, NT)
    n_att = 4 * lanes
    f_lanes = frame // 128
    for j in range(2 * f_lanes):
        r, l = j // f_lanes, j % f_lanes
        A[n_att + j] = back_t[r * 8 : r * 8 + 8, l * 128 : (l + 1) * 128]

    slab = nz * 24
    half_slab = slab // 2

    def term(ch):
        at = pl.ds(pl.multiple_of(ch * kc, kc), kc)
        return mm(dg[...], wg[at, :], NT) + mm(du[...], wu[at, :], NT) + mm(bk[...], a1[ch])

    def t_copy(k):
        return rcopy(TB.at[k], TR.at[k], t_s.at[k], t_r.at[k], dev_c)

    def x1_copy(k, which):
        if which == 0:
            return rcopy(
                SB.at[k, x2, pl.ds(0, half_slab)], XR1.at[k, 0], x1_s.at[k, 0], x1_r.at[k, 0], dev_xp
            )
        return rcopy(
            SB.at[k, x2, pl.ds(half_slab, half_slab)], XR1.at[k, 1], x1_s.at[k, 1], x1_r.at[k, 1], dev_xm
        )

    def x2_copy(k, which):
        if which == 0:
            return rcopy(SB.at[k, xp], XR2.at[k, 0], x2_s.at[k, 0], x2_r.at[k, 0], dev_xp)
        return rcopy(SB.at[k, xm], XR2.at[k, 1], x2_s.at[k, 1], x2_r.at[k, 1], dev_xm)

    def zz_copy(k, o):
        return rcopy(ZB.at[k, zpeer(o)], ZR.at[k, o - 1], zz_s.at[k, o - 1], zz_r.at[k, o - 1], dev_z(o))

    def e_copy(k, c_):
        return rcopy(EB.at[k, c_], E.at[s], e_s.at[k, c_], e_r.at[s], (dp_of(xx, zh, c_), core * nch + k))

    def e_local(k, c_):
        return pltpu.make_async_copy(EB.at[k, c_], E.at[s], e_l)

    def e_self(k, c_):
        return (core * nch + k == s) & (core == c_)

    def reduce_step(i, carry):
        @pl.when(i < nch)
        def _():
            k = i
            TB[k] = term(other * nch + k).astype(BF16)
            t_copy(k).start()
            own = term(core * nch + k)
            t_copy(k).wait_recv()
            total = own + TR[k].astype(F32)
            SB[k] = total.astype(BF16).reshape(NX, slab, kc)
            x1_copy(k, 0).start()
            x1_copy(k, 1).start()

        @pl.when((i >= 1) & (i < nch + 1))
        def _():
            k = i - 1
            for which, there, at in ((0, xp, 0), (1, xm, half_slab)):
                x1_copy(k, which).wait_recv()
                SB[k, there, at : at + half_slab] = (
                    SB[k, there, at : at + half_slab].astype(F32) + XR1[k, which].astype(F32)
                ).astype(BF16)
                x2_copy(k, which).start()

        @pl.when((i >= 2) & (i < nch + 2))
        def _():
            k = i - 2
            x2_copy(k, 0).wait_recv()
            x2_copy(k, 1).wait_recv()
            total = SB[k, xx].astype(F32) + XR2[k, 0].astype(F32) + XR2[k, 1].astype(F32)
            for z_ in range(nz):
                piece = total[z_ * 24 : z_ * 24 + 24]
                ZB[k, z_] = jnp.concatenate([piece[:, : kc // 2], piece[:, kc // 2 :]], axis=0).astype(BF16)
            for o in range(1, nz):
                zz_copy(k, o).start()

        @pl.when(i >= 3)
        def _():
            k = i - 3
            total = ZB[k, zh].astype(F32)
            for o in range(1, nz):
                zz_copy(k, o).wait_recv()
                total = total + ZR[k, o - 1].astype(F32)
            total = jnp.concatenate([total[0:24], total[24:48]], axis=1)
            EB[k, 0] = total[0:16].astype(BF16)
            EB[k, 1] = total[8:24].astype(BF16)
            for c_ in range(2):
                self_ = e_self(k, c_)

                @pl.when(self_)
                def _():
                    e_local(k, c_).start()
                    e_local(k, c_).wait()

                @pl.when(jnp.logical_not(self_))
                def _():
                    e_copy(k, c_).start()

        return carry

    lax.fori_loop(0, nch + 3, reduce_step, 0)

    def e_wait(o, carry):
        there = lax.rem(s + o, ns)
        rcopy(E.at[there], E.at[there], e_s.at[0, 0], e_r.at[there], dev_c).wait_recv()
        return carry

    lax.fori_loop(1, ns, e_wait, 0)
    home = s // nch == core

    @pl.when(jnp.logical_not(home))
    def _():
        rcopy(E.at[s], E.at[s], e_s.at[0, 0], e_r.at[s], dev_c).wait_recv()

    at = pl.ds(pl.multiple_of(s * kc, kc), kc)
    grad = mm(choose_all[:, 0 : 16 * ns], E[...].reshape(16 * ns, kc))
    spread = gain_ref[:, at] * grad
    hid_cols = hid_ref[:, at]
    hid_f = hid_cols.astype(F32)
    rad = rad_ref[:, 0:1]
    base = og_ref[:, at].astype(F32) + rad * spread
    stat_part = jnp.sum(spread * hid_f, axis=1, keepdims=True)
    PB[0:8, 0:toks] = jnp.broadcast_to(row_of(stat_part, toks), (8, toks))
    high, rest = two_parts(base)
    PB[8:24, 0:toks] = mm(att2_ref[...], high, NT) + mm(att2_ref[...], rest, NT)
    PB[24:40, 0:toks] = mm(att2_ref[...], hid_cols, NT)

    def q_copy(o):
        return rcopy(PB, PR.at[o - 1], q_s.at[o - 1], q_r.at[o - 1], (d, lax.rem(s + o, ns)))

    for o in range(1, ns):
        q_copy(o).start()
    total = PB[...]
    for o in range(1, ns):
        q_copy(o).wait_recv()
        total = total + PR[o - 1]
    stat_row = total[0:1, 0:toks] / width
    factor = rad * rad * rad * column(stat_row, toks)
    rg = (base - hid_f * factor).astype(BF16)
    rg_ref[...] = rg
    factor_row = row_of(factor, toks)
    back_low = (total[8:24, 0:toks] - total[24:40, 0:toks] * factor_row).astype(BF16)
    mixed_t = jnp.concatenate([total[40:64, :], jnp.zeros((104, 128), F32)], axis=0).T
    mixed_low = mixed_t[0:16, 0:toks].astype(BF16)
    first = SCALE * mm(back_low, mix_ref[...])
    second = SCALE * mm(mixed_low, rg)
    for j in range(lanes):
        cols = slice(j * 128, (j + 1) * 128)
        A[j] = first[0:8, cols]
        A[lanes + j] = first[8:16, cols]
        A[2 * lanes + j] = second[0:8, cols]
        A[3 * lanes + j] = second[8:16, cols]

    def a_copy(o):
        to = lax.rem(d + o, nd)
        return rcopy(A.at[to], AR.at[o - 1], a_s.at[o - 1], a_r.at[o - 1], (to, s))

    def f_copy(o):
        to = lax.rem(d + o, nd)
        return rcopy(F.at[d], F.at[d], f_s.at[o - 1], f_r.at[d], (to, s))

    def a_start(o, carry):
        a_copy(o).start()
        return carry

    lax.fori_loop(1, nd, a_start, 0)

    def a_add(o, tile):
        a_copy(o).wait_recv()
        return tile + AR[o - 1]

    F[d] = lax.fori_loop(1, nd, a_add, A[d])

    def f_start(o, carry):
        f_copy(o).start()
        return carry

    lax.fori_loop(1, nd, f_start, 0)

    def f_wait(o, carry):
        frm = lax.rem(d + o, nd)
        rcopy(F.at[frm], F.at[frm], f_s.at[0], f_r.at[frm], dev_c).wait_recv()
        return carry

    lax.fori_loop(1, nd, f_wait, 0)

    for j in range(lanes):
        cols = slice(j * 128, (j + 1) * 128)
        af_ref[0:8, cols] = F[j]
        af_ref[8:16, cols] = F[lanes + j]
        as_ref[0:8, cols] = F[2 * lanes + j]
        as_ref[8:16, cols] = F[3 * lanes + j]
    back_full = jnp.concatenate(
        [
            jnp.concatenate([F[n_att + r * f_lanes + l] for l in range(f_lanes)], axis=1)
            for r in range(2)
        ],
        axis=0,
    )
    high, rest = two_parts(back_full)
    both = jnp.concatenate([high, rest], axis=0)

    def first_gradient(ch, carry):
        xrows = G[ch, :, 0:32, :].reshape(frame, kc)
        pair = mm(both, xrows)
        ga_ref[:, pl.ds(pl.multiple_of(ch * kc, kc), kc)] = pair[0:16] + pair[16:32]
        return carry

    lax.fori_loop(0, 2 * nch, first_gradient, 0)

    swap.wait_send()

    def drain(k, carry):
        for o in range(1, nz):
            z_copy(k, o).wait_send()
            zz_copy(k, o).wait_send()
        for which in range(4):
            x_copy(k, which).wait_send()
        c_copy(k).wait_send()
        t_copy(k).wait_send()
        for which in range(2):
            x1_copy(k, which).wait_send()
            x2_copy(k, which).wait_send()
        for c_ in range(2):

            @pl.when(jnp.logical_not(e_self(k, c_)))
            def _():
                e_copy(k, c_).wait_send()

        return carry

    lax.fori_loop(0, nch, drain, 0)
    for o in range(1, ns):
        q_copy(o).wait_send()

    def drain_dp(o, carry):
        a_copy(o).wait_send()
        f_copy(o).wait_send()
        return carry

    lax.fori_loop(1, nd, drain_dp, 0)


def fused(nz, ns, *args):
    hid, mix = args[0], args[1]
    width, kc = hid.shape[1], mix.shape[1]
    toks = hid.shape[0]
    hidden = args[6].shape[1]
    nch = ns // 2
    nd = NX * nz * 2
    chips = NX * nz
    rows, frame = chips * 24, chips * 32
    slab = nz * 24
    zo = max(nz - 1, 1)
    vm = pltpu.VMEM
    dma = pltpu.SemaphoreType.DMA
    scratch = [
        vm((width, hidden), BF16),
        vm((width, hidden), BF16),
        vm((2 * nch, hidden, kc), BF16),
        vm((2 * nch, 16, kc), BF16),
        vm((nch, 48, kc), BF16),
        vm((2 * nch, 48, kc), BF16),
        vm((2 * nch, chips, 48, kc), BF16),
        vm((frame, hidden), F32),
        vm((frame, hidden), F32),
        vm((frame, hidden), F32),
        vm((frame, 128), F32),
        vm((rows, hidden), BF16),
        vm((rows, hidden), BF16),
        vm((rows, 16), BF16),
        vm((nch, rows, kc), BF16),
        vm((nch, rows, kc), BF16),
        vm((nch, NX, slab, kc), BF16),
        vm((nch, 2, slab // 2, kc), BF16),
        vm((nch, 2, slab, kc), BF16),
        vm((nch, nz, 48, kc // 2), BF16),
        vm((nch, zo, 48, kc // 2), BF16),
        vm((nch, 2, 16, kc), BF16),
        vm((ns, 16, kc), BF16),
        vm((64, 128), F32),
        vm((ns - 1, 64, 128), F32),
        vm((nd, 8, 128), F32),
        vm((nd - 1, 8, 128), F32),
        vm((nd, 8, 128), F32),
        vm((toks, 128), F32),
        dma((3 + 2 * nch,)),
        dma,
        dma,
        dma((nch, zo)),
        dma((nch, zo)),
        dma((nch, 4)),
        dma((nch, 4)),
        dma((nch,)),
        dma((nch,)),
        dma((nch,)),
        dma((nch,)),
        dma((nch, 2)),
        dma((nch, 2)),
        dma((nch, 2)),
        dma((nch, 2)),
        dma((nch, zo)),
        dma((nch, zo)),
        dma((nch, 2)),
        dma((ns,)),
        dma,
        dma((ns - 1,)),
        dma((ns - 1,)),
        dma((nd - 1,)),
        dma((nd - 1,)),
        dma((nd - 1,)),
        dma((nd,)),
    ]
    vmem = pl.BlockSpec(memory_space=pltpu.VMEM)
    hbm = pl.BlockSpec(memory_space=pl.ANY)
    return pl.pallas_call(
        functools.partial(kernel, nz, ns, kc),
        out_shape=(
            jax.ShapeDtypeStruct((toks, kc), BF16),
            jax.ShapeDtypeStruct((16, width), F32),
            jax.ShapeDtypeStruct((16, hidden), F32),
            jax.ShapeDtypeStruct((16, kc), F32),
            jax.ShapeDtypeStruct((16, kc), F32),
        ),
        in_specs=[vmem] * 6 + [hbm] * 4 + [vmem] * 3,
        out_specs=(vmem,) * 5,
        scratch_shapes=scratch,
        compiler_params=pltpu.CompilerParams(
            collective_id=0, has_side_effects=True, vmem_limit_bytes=58 * 1024 * 1024
        ),
        cost_estimate=pl.CostEstimate(
            flops=2 * rows * width * hidden * 5, bytes_accessed=6 * width * hidden, transcendentals=0
        ),
    )(*args)


def body(nz, hid, mix, og, gain, routes, rw, wg, wu, wd, a1, a2, att1, att2):
    ns = lax.axis_size("shard")
    width, kc = hid.shape[1], mix.shape[1]
    a1_chunks = a1[0].T.reshape(16, ns, kc).swapaxes(0, 1)
    rg, ga, gs, af, sec = fused(
        nz,
        ns,
        hid,
        mix,
        og,
        gain.reshape(1, width),
        routes.T,
        rw.T,
        wg[0],
        wu[0],
        wd[0],
        a1_chunks,
        a2[0],
        att1.T,
        att2,
    )
    return rg, ga.T[None], gs[None], af.T, sec


def solution(mesh):
    nz = mesh.shape["dp"] // (2 * NX)
    in_specs = (
        P("dp", None),
        P("dp", "shard"),
        P("dp", None),
        P(),
        P("dp", None),
        P("dp", None),
        P("shard", None, "dp"),
        P("shard", None, "dp"),
        P("shard", "dp", None),
        P("shard", None, None),
        P("shard", None, "dp"),
        P("shard", None),
        P(None, "shard"),
    )
    out_specs = (
        P("dp", "shard"),
        P("shard", None, None),
        P("shard", None, "dp"),
        P("shard", None),
        P(None, "shard"),
    )
    return jax.shard_map(
        functools.partial(body, nz), mesh=mesh, in_specs=in_specs, out_specs=out_specs, check_vma=False
    )
```

```python
import functools

import jax
import jax.numpy as jnp
from jax import lax
from jax.experimental import pallas as pl
from jax.experimental.pallas import tpu as pltpu
from jax.sharding import PartitionSpec as P

CAP = 12
EPSILON = 1e-05
SCALE = 0.5
NX = 4
F32 = jnp.float32
BF16 = jnp.bfloat16
MESH = pl.DeviceIdType.MESH
NN = (((1,), (0,)), ((), ()))
NT = (((1,), (1,)), ((), ()))


def mm(a, b, dims=NN):
    return lax.dot_general(a, b, dims, preferred_element_type=F32)


def two_parts(value):
    high = value.astype(BF16)
    return high, (value - high.astype(F32)).astype(BF16)


def column(row, count):
    eye = lax.broadcasted_iota(jnp.int32, (count, count), 0) == lax.broadcasted_iota(
        jnp.int32, (count, count), 1
    )
    return jnp.sum(jnp.where(eye, jnp.broadcast_to(row, (count, count)), 0.0), axis=1, keepdims=True)


def row_of(col, count):
    eye = lax.broadcasted_iota(jnp.int32, (count, count), 0) == lax.broadcasted_iota(
        jnp.int32, (count, count), 1
    )
    return jnp.sum(jnp.where(eye, jnp.broadcast_to(col, (count, count)), 0.0), axis=0, keepdims=True)


def kernel(
    nz,
    ns,
    kc,
    hid_ref,
    mix_ref,
    og_ref,
    gain_ref,
    routes_ref,
    rw_ref,
    wg_hbm,
    wu_hbm,
    wd_hbm,
    a1_hbm,
    a2_ref,
    att1_ref,
    att2_ref,
    rg_ref,
    ga_ref,
    gs_ref,
    af_ref,
    as_ref,
    wg,
    wu,
    wd,
    a1,
    rb,
    sb0,
    G,
    acc_g,
    acc_u,
    acc_d,
    acc_l,
    dg,
    du,
    bk,
    TB,
    TR,
    SB,
    XR1,
    XR2,
    ZB,
    ZR,
    EB,
    E,
    PB,
    PR,
    at_bufs,
    bk_bufs,
    rad_ref,
    w_sem,
    p0_s,
    p0_r,
    g_s,
    s1_r,
    s2_r,
    c_s,
    c_r,
    t_s,
    t_r,
    x_s,
    x1_r,
    x2_r,
    zz_s,
    zz_r,
    e_s,
    e_r,
    e_l,
    q_s,
    q_r,
    at_sems,
    bk_sems,
):
    nch = ns // 2
    nd = NX * nz * 2
    chips = NX * nz
    toks = hid_ref.shape[0]
    width = hid_ref.shape[1]
    hw = width // 2
    frame = chips * 32
    rows = chips * 24
    lanes = kc // 128
    d = lax.axis_index("dp")
    s = lax.axis_index("shard")
    core = lax.rem(d, 2)
    zh = lax.rem(d // 2, nz)
    xx = d // (2 * nz)
    q = xx * nz + zh
    other = 1 - core

    def dp_of(x_, z_, c_):
        return (x_ * nz + z_) * 2 + c_

    xp, xm, x2 = lax.rem(xx + 1, NX), lax.rem(xx + 3, NX), lax.rem(xx + 2, NX)
    dev_c = (dp_of(xx, zh, other), s)
    dev_xp = (dp_of(xp, zh, core), s)
    dev_xm = (dp_of(xm, zh, core), s)

    def zpeer(o):
        return lax.rem(zh + o, nz)

    def dev_z(o):
        return (dp_of(xx, zpeer(o), core), s)

    def rcopy(src, dst, ssem, rsem, dev):
        return pltpu.make_async_remote_copy(
            src_ref=src, dst_ref=dst, send_sem=ssem, recv_sem=rsem, device_id=dev, device_id_type=MESH
        )

    w_copies = [
        pltpu.make_async_copy(wg_hbm, wg, w_sem.at[0]),
        pltpu.make_async_copy(wu_hbm, wu, w_sem.at[1]),
    ] + [
        pltpu.make_async_copy(wd_hbm.at[:, pl.ds(i * kc, kc)], wd.at[i], w_sem.at[2 + i])
        for i in range(2 * nch)
    ] + [
        pltpu.make_async_copy(a1_hbm.at[:, pl.ds(i * kc, kc)], a1.at[i], w_sem.at[2 + 2 * nch + i])
        for i in range(2 * nch)
    ]
    for copy in w_copies:
        copy.start()

    barrier = pltpu.get_barrier_semaphore()

    def greet(dev):
        pl.semaphore_signal(barrier, inc=1, device_id=dev, device_id_type=MESH)

    group = [(dc, o) for dc in range(2) for o in range(NX)][1:]

    def dev_g(dc, o):
        return (dp_of(lax.rem(xx + o, NX), zh, other if dc else core), s)

    for dc, o in group:
        greet(dev_g(dc, o))
    for o in range(1, nz):
        greet(dev_z(o))

    def greet_shard(o, carry):
        there = lax.rem(s + o, ns)
        greet((d, there))
        greet((dp_of(xx, zh, other), there))
        return carry

    lax.fori_loop(1, ns, greet_shard, 0)

    hid = hid_ref[...].astype(F32)
    radius = lax.rsqrt(jnp.mean(hid * hid, axis=1, keepdims=True) + EPSILON)
    rad_ref[...] = jnp.broadcast_to(radius, rad_ref.shape)
    normed = hid * radius * gain_ref[...]
    tok = jnp.concatenate([normed, og_ref[...].astype(F32)], axis=0).astype(BF16)

    r0 = column(routes_ref[0:1, :].astype(F32), toks)
    r1 = column(routes_ref[1:2, :].astype(F32), toks)
    w0 = column(rw_ref[0:1, :], toks)
    w1 = column(rw_ref[1:2, :], toks)
    lane = lax.broadcasted_iota(jnp.int32, (toks, 128), 1)
    lower = (
        lax.broadcasted_iota(jnp.int32, (toks, toks), 0) > lax.broadcasted_iota(jnp.int32, (toks, toks), 1)
    ).astype(F32).astype(BF16)
    lane_e = (lane // 16).astype(F32)
    named_all = jnp.where((r0 == lane_e) | (r1 == lane_e), 1.0, 0.0)
    slot_all = mm(lower, named_all.astype(BF16))
    place_f = lax.rem(lane, 16).astype(F32)
    choose_all = jnp.where(slot_all + (4 * core).astype(F32) == place_f, named_all, 0.0).astype(BF16)
    mine = jnp.broadcast_to(s.astype(F32), (toks, 128))
    hit0 = jnp.where(r0 == mine, 1.0, 0.0)
    hit1 = jnp.where(r1 == mine, 1.0, 0.0)
    named = hit0 + hit1
    weight = hit0 * w0 + hit1 * w1
    slot = mm(lower, named.astype(BF16)) + (CAP * core).astype(F32)
    row_x = jnp.where(lane < 24, lane, -1).astype(F32)
    row_y = jnp.where(
        (lane >= 24) & (lane < 32), lane - 8, jnp.where((lane >= 32) & (lane < 48), lane - 32, -1)
    ).astype(F32)
    hot_x = jnp.where(slot == row_x, named, 0.0)
    hot_y = jnp.where(slot == row_y, named, 0.0)
    blank = jnp.zeros((128 - 2 * toks, 128), F32)
    hot = jnp.concatenate([hot_x, hot_y, blank], axis=0).T
    scale = jnp.concatenate([hot_x, hot_y * weight, blank], axis=0).T
    hot = hot[0:48, 0:48].astype(BF16)
    scale = jnp.sum(scale[0:48, :], axis=1, keepdims=True)
    for j in range(2 * nch):
        part = mm(hot, tok[:, j * kc : (j + 1) * kc]) * scale
        sb0[j] = part.astype(BF16)

    pl.semaphore_wait(barrier, 2 * NX - 1 + nz - 1 + 2 * (ns - 1))

    swap = rcopy(sb0.at[pl.ds(other * nch, nch)], rb, p0_s, p0_r, dev_c)
    swap.start()

    mix_f = mix_ref[...].astype(F32)
    mix_rows = jnp.concatenate([jnp.zeros((96, kc), F32), mix_f, jnp.zeros((8, kc), F32)], axis=0)
    PB[8:24] = mm(att1_ref[...], mix_rows.astype(BF16), NT)

    class Sum:
        def __init__(self, bufs, sems):
            self.part, self.g_in, self.z_in, self.full = bufs
            self.send, self.g_r, self.z_r, self.b_r = sems
            self.n8 = self.part.shape[2]

        def where(self, t):
            return t // (4 * self.n8), (t // self.n8) % 4, t % self.n8

        def put(self, t, tile):
            self.part[self.where(t)] = tile

        def get(self, t):
            return self.full[self.where(t)]

        def g_copy(self, m):
            dc, o = group[m]
            src = self.part.at[other if dc else core, lax.rem(xx + o, NX)]
            return rcopy(src, self.g_in.at[m], self.send.at[m], self.g_r.at[m], dev_g(dc, o))

        def z_copy(self, o):
            ref = self.z_in.at[zh]
            return rcopy(ref, ref, self.send.at[6 + o], self.z_r.at[o - 1], dev_z(o))

        def b_copy(self, m):
            ref = self.full.at[core, xx]
            return rcopy(ref, ref, self.send.at[10 + m], self.b_r.at[m], dev_g(*group[m]))

        def step(self, n):
            if n == 0:
                for m in range(7):
                    self.g_copy(m).start()
            elif n == 1:
                total = self.part[core, xx]
                for m in range(7):
                    self.g_copy(m).wait_recv()
                    total = total + self.g_in[m]
                self.z_in[zh] = total
                for o in range(1, 4):
                    self.z_copy(o).start()
            elif n == 2:
                for o in range(1, 4):
                    self.z_copy(o).wait_recv()
                self.full[core, xx] = self.z_in[0] + self.z_in[1] + self.z_in[2] + self.z_in[3]
                for m in range(7):
                    self.b_copy(m).start()
            else:
                for m in range(7):
                    self.b_copy(m).wait_recv()

        def sent(self):
            for m in range(7):
                self.g_copy(m).wait_send()
                self.b_copy(m).wait_send()
            for o in range(1, 4):
                self.z_copy(o).wait_send()

    att_sum = Sum(at_bufs, at_sems)
    back_sum = Sum(bk_bufs, bk_sems)

    acc_g[...] = jnp.zeros_like(acc_g)
    acc_u[...] = jnp.zeros_like(acc_u)
    acc_d[...] = jnp.zeros_like(acc_d)
    acc_l[...] = jnp.zeros_like(acc_l)

    swap.wait_recv()

    zm, zp, z2 = lax.rem(zh + 3, nz), lax.rem(zh + 1, nz), lax.rem(zh + 2, nz)
    dev_zp, dev_zm = dev_z(1), dev_z(3)
    last = nch - 1
    xs_of, zs_of = (xx, xm, xp, x2), (zh, zm, zp, z2)

    def along(k, first):
        return (k != last) == first

    def ring(k, on_z, fixed, which, ssem, rsem):
        ch = core * nch + k
        if on_z:
            at, low_, high_, up, down = fixed * nz + zh, fixed * nz + zm, fixed * nz + zp, dev_zp, dev_zm
        else:
            at, low_, high_, up, down = xx * nz + fixed, xm * nz + fixed, xp * nz + fixed, dev_xp, dev_xm
        if which == 0:
            ref, dev = G.at[ch, at], up
        elif which == 1:
            ref, dev = G.at[ch, at], down
        elif which == 2:
            ref, dev = G.at[ch, low_, :, pl.ds(0, kc // 2)], up
        else:
            ref, dev = G.at[ch, high_, :, pl.ds(kc // 2, kc // 2)], down
        return rcopy(ref, ref, ssem, rsem, dev)

    def s1(k, which):
        on_z = along(k, True)
        return ring(k, on_z, xx if on_z else zh, which, g_s.at[k], s1_r.at[k, which])

    def s2(k, p, which):
        on_z = along(k, False)
        fixed = xs_of[p] if on_z else zs_of[p]
        return ring(k, on_z, fixed, which, g_s.at[k], s2_r.at[k, p, which])

    def c_copy(k, p=None):
        if p is None:
            ref, n = G.at[core * nch + k], 0
        else:
            ref, n = G.at[core * nch + k, pl.ds(xs_of[p] * nz, nz)], p
        return rcopy(ref, ref, c_s.at[k, n], c_r.at[k, n], dev_c)

    def piece(k):
        G[core * nch + k, q] = (sb0[core * nch + k].astype(F32) + rb[k].astype(F32)).astype(BF16)

    def s2_out(k, p):
        s2(k, p, 0).start()
        s2(k, p, 1).start()

    def s1_pass(k):
        for which in range(2):
            s1(k, which).wait_recv()
            s1(k, 2 + which).start()
            if k != last:
                s2_out(k, 1 + which)

    def s1_far(k):
        s1(k, 2).wait_recv()
        s1(k, 3).wait_recv()
        s2_out(k, 3)

    def s2_pass(k, p):
        for which in range(2):
            s2(k, p, which).wait_recv()
            s2(k, p, 2 + which).start()

    def s2_done(k):
        for p in range(4):
            s2(k, p, 2).wait_recv()
            s2(k, p, 3).wait_recv()
            if k == last:
                c_copy(k, p).start()
        if k != last:
            c_copy(k).start()

    def product(ch):
        xrows = G[ch, :, 0:32, :].reshape(frame, kc)
        yrows = G[ch, :, 16:48, :].reshape(frame, kc)
        at = pl.ds(pl.multiple_of(ch * kc, kc), kc)
        acc_g[...] += mm(xrows, wg[at, :])
        acc_u[...] += mm(xrows, wu[at, :])
        acc_l[:, 0:16] += mm(xrows, a1[ch], NT)
        acc_d[...] += mm(yrows, wd[ch], NT)

    def of_other(k):
        if k == last:
            for p in range(4):
                c_copy(k, p).wait_recv()
        else:
            c_copy(k).wait_recv()
        product(other * nch + k)

    def s1_out(k):
        s1(k, 0).start()
        s1(k, 1).start()

    piece(last)
    s1_out(last)
    piece(0)
    s1_out(0)
    s2_out(0, 0)
    piece(1)
    s1_out(1)
    piece(2)
    s1_pass(last)
    s2_out(1, 0)
    s2_pass(0, 0)
    s1_pass(0)
    s1_out(2)
    s2_pass(1, 0)
    s1_pass(1)
    s1_far(0)
    s2_out(2, 0)
    s2_pass(0, 1)
    s2_pass(0, 2)
    s2_out(last, 0)
    s1_pass(2)
    s1_far(1)
    s2_out(last, 1)
    s2_pass(0, 3)
    s2_pass(2, 0)
    s1_far(2)
    s2_out(last, 2)
    s2_pass(1, 1)
    s2_pass(1, 2)
    s1_far(last)
    for copy in w_copies:
        copy.wait()
    s2_done(0)
    product(core * nch)
    s2_pass(last, 0)
    s2_pass(1, 3)
    s2_pass(last, 1)
    s2_pass(2, 1)
    s2_pass(2, 2)
    of_other(0)
    s2_done(1)
    product(core * nch + 1)
    s2_pass(last, 2)
    s2_pass(2, 3)
    s2_pass(last, 3)
    of_other(1)
    s2_done(2)
    product(core * nch + 2)
    of_other(2)
    s2_done(last)
    product(core * nch + last)
    of_other(last)

    low = acc_l[...].astype(BF16)
    gate = acc_g[...] + SCALE * mm(low[:, 0:16], a2_ref[...])
    hidden = gate.shape[1]
    gate = gate.reshape(chips, 32, hidden)[:, 0:24, :]
    upper = acc_u[...].reshape(chips, 32, hidden)[:, 0:24, :]
    dact = acc_d[...].reshape(chips, 32, hidden)
    dact = jnp.concatenate([dact[:, 16:32, :], dact[:, 8:16, :]], axis=1)
    sig = 1.0 / (1.0 + jnp.exp(-gate))
    dgate = dact * upper * sig * (1.0 + gate * (1.0 - sig))
    dup = dact * gate * sig
    du[...] = dup.reshape(rows, hidden).astype(BF16)
    dgate_rows = dgate.reshape(rows, hidden).astype(BF16)
    dg[...] = dgate_rows
    bk[...] = (SCALE * mm(dgate_rows, a2_ref[...], NT)).astype(BF16)
    dgate_frame = (
        jnp.concatenate([dgate, jnp.zeros((chips, 8, hidden), F32)], axis=1)
        .reshape(frame, hidden)
        .astype(BF16)
    )
    low_t = acc_l[...].T[0:16, :].astype(BF16)
    gs_ref[...] = SCALE * mm(low_t, dgate_frame)
    back_t = SCALE * mm(a2_ref[...], dgate_frame, NT)
    f_lanes = frame // 128
    n_back = 2 * f_lanes
    for j in range(n_back):
        r, l = j // f_lanes, j % f_lanes
        back_sum.put(j, back_t[r * 8 : r * 8 + 8, l * 128 : (l + 1) * 128])

    back_sum.step(0)

    slab = nz * 24
    half_slab = slab // 2

    hc = kc // 2

    def term(half, j):
        ch = half * nch + j // 2
        at = pl.ds(pl.multiple_of(ch * kc + (j % 2) * hc, hc), hc)
        cols = slice((j % 2) * hc, (j % 2) * hc + hc)
        return mm(dg[...], wg[at, :], NT) + mm(du[...], wu[at, :], NT) + mm(bk[...], a1[ch, :, cols])

    def t_copy(k):
        return rcopy(TB.at[k], TR.at[k], t_s.at[k], t_r.at[k], dev_c)

    def x1_copy(k, which):
        if which == 0:
            return rcopy(
                SB.at[k, x2, pl.ds(0, half_slab)], XR1.at[k, 0], x_s.at[k], x1_r.at[k, 0], dev_xp
            )
        return rcopy(
            SB.at[k, x2, pl.ds(half_slab, half_slab)], XR1.at[k, 1], x_s.at[k], x1_r.at[k, 1], dev_xm
        )

    def x2_copy(k, which):
        if which == 0:
            return rcopy(SB.at[k, xp], XR2.at[k, 0], x_s.at[k], x2_r.at[k, 0], dev_xp)
        return rcopy(SB.at[k, xm], XR2.at[k, 1], x_s.at[k], x2_r.at[k, 1], dev_xm)

    def zz_copy(k, o):
        return rcopy(ZB.at[k, zpeer(o)], ZR.at[k, o - 1], zz_s.at[k], zz_r.at[k, o - 1], dev_z(o))

    def e_copy(k, c_):
        return rcopy(EB.at[k, c_], E.at[s], e_s.at[k, c_], e_r.at[s], (dp_of(xx, zh, c_), core * nch + k))

    def e_local(k, c_):
        return pltpu.make_async_copy(EB.at[k, c_], E.at[s], e_l)

    def e_self(k, c_):
        return (core * nch + k == s) & (core == c_)

    def send_term(j):
        TB[j] = term(other, j).astype(BF16)
        t_copy(j).start()

    def core_sum(j):
        own = term(core, j)
        t_copy(j).wait_recv()
        SB[j] = (own + TR[j].astype(F32)).astype(BF16).reshape(NX, slab, hc)
        x1_copy(j, 0).start()
        x1_copy(j, 1).start()

    def x_pass(j):
        for which, there, at in ((0, xp, 0), (1, xm, half_slab)):
            x1_copy(j, which).wait_recv()
            SB[j, there, at : at + half_slab] = (
                SB[j, there, at : at + half_slab].astype(F32) + XR1[j, which].astype(F32)
            ).astype(BF16)
            x2_copy(j, which).start()

    def x_sum(j):
        x2_copy(j, 0).wait_recv()
        x2_copy(j, 1).wait_recv()
        return SB[j, xx].astype(F32) + XR2[j, 0].astype(F32) + XR2[j, 1].astype(F32)

    def z_send(k):
        left, right = x_sum(2 * k), x_sum(2 * k + 1)
        for z_ in range(nz):
            rows_ = slice(z_ * 24, z_ * 24 + 24)
            ZB[k, z_] = jnp.concatenate([left[rows_], right[rows_]], axis=0).astype(BF16)
        for o in range(1, nz):
            zz_copy(k, o).start()

    def z_sum(k):
        total = ZB[k, zh].astype(F32)
        for o in range(1, nz):
            zz_copy(k, o).wait_recv()
            total = total + ZR[k, o - 1].astype(F32)
        total = jnp.concatenate([total[0:24], total[24:48]], axis=1)
        EB[k, 0] = total[0:16].astype(BF16)
        EB[k, 1] = total[8:24].astype(BF16)
        for c_ in range(2):
            self_ = e_self(k, c_)

            @pl.when(self_)
            def _():
                e_local(k, c_).start()
                e_local(k, c_).wait()

            @pl.when(jnp.logical_not(self_))
            def _():
                e_copy(k, c_).start()

    send_term(0)
    for j in range(2 * nch + 8):
        if j + 1 < 2 * nch:
            send_term(j + 1)
        if j < 2 * nch:
            core_sum(j)
        if j in (2, 4):
            back_sum.step(j // 2)
        if 0 <= j - 2 < 2 * nch:
            x_pass(j - 2)
        at = j - 4
        if at % 2 == 1 and 0 <= at // 2 < nch:
            z_send(at // 2)
        at = j - 6
        if at % 2 == 1 and 0 <= at // 2 < nch:
            z_sum(at // 2)
    back_sum.step(3)

    def e_wait(o, carry):
        there = lax.rem(s + o, ns)
        rcopy(E.at[there], E.at[there], e_s.at[0, 0], e_r.at[there], dev_c).wait_recv()
        return carry

    lax.fori_loop(1, ns, e_wait, 0)
    home = s // nch == core

    @pl.when(jnp.logical_not(home))
    def _():
        rcopy(E.at[s], E.at[s], e_s.at[0, 0], e_r.at[s], dev_c).wait_recv()

    at = pl.ds(pl.multiple_of(s * kc, kc), kc)
    grad = mm(choose_all[:, 0 : 16 * ns], E[...].reshape(16 * ns, kc))
    spread = gain_ref[:, at] * grad
    hid_cols = hid_ref[:, at]
    hid_f = hid_cols.astype(F32)
    rad = rad_ref[:, 0:1]
    base = og_ref[:, at].astype(F32) + rad * spread
    stat_part = jnp.sum(spread * hid_f, axis=1, keepdims=True)
    PB[0:8, 0:toks] = jnp.broadcast_to(row_of(stat_part, toks), (8, toks))
    high, rest = two_parts(base)
    gap = jnp.zeros((8, kc), F32)
    stack = jnp.concatenate(
        [high.astype(F32), gap, rest.astype(F32), gap, hid_f, gap, jnp.zeros((32, kc), F32)], axis=0
    )
    PB[8:24] = PB[8:24] + mm(att2_ref[...], stack.astype(BF16), NT)

    def q_copy(o):
        return rcopy(PB, PR.at[o - 1], q_s, q_r.at[o - 1], (d, lax.rem(s + o, ns)))

    for o in range(1, ns):
        q_copy(o).start()
    total = PB[...]
    for o in range(1, ns):
        q_copy(o).wait_recv()
        total = total + PR[o - 1]
    stat_row = total[0:1, 0:toks] / width
    factor = rad * rad * rad * column(stat_row, toks)
    rg = (base - hid_f * factor).astype(BF16)
    rg_ref[...] = rg
    factor_row = row_of(factor, toks)
    low_parts = total[8:24, :]
    back_low = (
        low_parts[:, 0:toks] + low_parts[:, 32 : 32 + toks] - low_parts[:, 64 : 64 + toks] * factor_row
    ).astype(BF16)
    mixed_low = low_parts[:, 96 : 96 + toks].astype(BF16)
    first = SCALE * mm(back_low, mix_ref[...])
    second = SCALE * mm(mixed_low, rg)
    for j in range(lanes):
        cols = slice(j * 128, (j + 1) * 128)
        att_sum.put(j, first[0:8, cols])
        att_sum.put(lanes + j, first[8:16, cols])
        att_sum.put(2 * lanes + j, second[0:8, cols])
        att_sum.put(3 * lanes + j, second[8:16, cols])
    att_sum.step(0)

    back_full = jnp.concatenate(
        [
            jnp.concatenate([back_sum.get(r * f_lanes + l) for l in range(f_lanes)], axis=1)
            for r in range(2)
        ],
        axis=0,
    )
    high, rest = two_parts(back_full)
    both = jnp.concatenate([high, rest], axis=0)

    def first_gradient(ch, carry):
        xrows = G[ch, :, 0:32, :].reshape(frame, kc)
        pair = mm(both, xrows)
        ga_ref[:, pl.ds(pl.multiple_of(ch * kc, kc), kc)] = pair[0:16] + pair[16:32]
        return carry

    lax.fori_loop(0, 3, first_gradient, 0)
    att_sum.step(1)
    lax.fori_loop(3, 6, first_gradient, 0)
    att_sum.step(2)
    lax.fori_loop(6, 2 * nch, first_gradient, 0)

    swap.wait_send()

    def drain(k, carry):
        sent = G.at[k, pl.ds(0, 15)]
        rcopy(sent, sent, g_s.at[k], g_s.at[k], dev_c).wait_send()
        sent = ZB.at[k, pl.ds(0, nz - 1)]
        rcopy(sent, sent, zz_s.at[k], zz_s.at[k], dev_c).wait_send()
        for j in range(2):
            t_copy(2 * k + j).wait_send()
            sent = TB.at[2 * k + j, pl.ds(0, 3 * slab)]
            rcopy(sent, sent, x_s.at[2 * k + j], x_s.at[2 * k + j], dev_c).wait_send()
        for c_ in range(2):

            @pl.when(jnp.logical_not(e_self(k, c_)))
            def _():
                e_copy(k, c_).wait_send()

        return carry

    lax.fori_loop(0, nch, drain, 0)
    for k in range(last):
        c_copy(k).wait_send()
    for p in range(4):
        c_copy(last, p).wait_send()
    rcopy(PR, PR, q_s, q_s, dev_c).wait_send()
    back_sum.sent()

    att_sum.step(3)
    for j in range(lanes):
        cols = slice(j * 128, (j + 1) * 128)
        af_ref[0:8, cols] = att_sum.get(j)
        af_ref[8:16, cols] = att_sum.get(lanes + j)
        as_ref[0:8, cols] = att_sum.get(2 * lanes + j)
        as_ref[8:16, cols] = att_sum.get(3 * lanes + j)
    att_sum.sent()


def hand_on(*refs):
    count = len(refs) // 2
    for i in range(count):
        refs[count + i][...] = refs[i][...]


def fused(nz, ns, *args):
    hid, mix = args[0], args[1]
    width, kc = hid.shape[1], mix.shape[1]
    toks = hid.shape[0]
    hidden = args[6].shape[1]
    nch = ns // 2
    nd = NX * nz * 2
    chips = NX * nz
    rows, frame = chips * 24, chips * 32
    slab = nz * 24
    zo = max(nz - 1, 1)
    vm = pltpu.VMEM
    dma = pltpu.SemaphoreType.DMA
    sum_sems = (dma((17,)), dma((7,)), dma((3,)), dma((7,)))

    def tiles(count):
        n8 = count // 8
        return (
            vm((2, 4, n8, 8, 128), F32),
            vm((7, n8, 8, 128), F32),
            vm((4, n8, 8, 128), F32),
            vm((2, 4, n8, 8, 128), F32),
        )

    scratch = [
        vm((width, hidden), BF16),
        vm((width, hidden), BF16),
        vm((2 * nch, hidden, kc), BF16),
        vm((2 * nch, 16, kc), BF16),
        vm((nch, 48, kc), BF16),
        vm((2 * nch, 48, kc), BF16),
        vm((2 * nch, chips, 48, kc), BF16),
        vm((frame, hidden), F32),
        vm((frame, hidden), F32),
        vm((frame, hidden), F32),
        vm((frame, 128), F32),
        vm((rows, hidden), BF16),
        vm((rows, hidden), BF16),
        vm((rows, 16), BF16),
        vm((2 * nch, rows, kc // 2), BF16),
        vm((2 * nch, rows, kc // 2), BF16),
        vm((2 * nch, NX, slab, kc // 2), BF16),
        vm((2 * nch, 2, slab // 2, kc // 2), BF16),
        vm((2 * nch, 2, slab, kc // 2), BF16),
        vm((nch, nz, 48, kc // 2), BF16),
        vm((nch, zo, 48, kc // 2), BF16),
        vm((nch, 2, 16, kc), BF16),
        vm((ns, 16, kc), BF16),
        vm((24, 128), F32),
        vm((ns - 1, 24, 128), F32),
        tiles(4 * kc // 128),
        tiles(2 * frame // 128),
        vm((toks, 128), F32),
        dma((2 + 4 * nch,)),
        dma,
        dma,
        dma((nch,)),
        dma((nch, 4)),
        dma((nch, 4, 4)),
        dma((nch, 4)),
        dma((nch, 4)),
        dma((2 * nch,)),
        dma((2 * nch,)),
        dma((2 * nch,)),
        dma((2 * nch, 2)),
        dma((2 * nch, 2)),
        dma((nch,)),
        dma((nch, zo)),
        dma((nch, 2)),
        dma((ns,)),
        dma,
        dma,
        dma((ns - 1,)),
        sum_sems,
        sum_sems,
    ]
    vmem = pl.BlockSpec(memory_space=pltpu.VMEM)
    hbm = pl.BlockSpec(memory_space=pl.ANY)
    results = pl.pallas_call(
        functools.partial(kernel, nz, ns, kc),
        out_shape=(
            jax.ShapeDtypeStruct((toks, kc), BF16),
            jax.ShapeDtypeStruct((16, width), F32),
            jax.ShapeDtypeStruct((16, hidden), F32),
            jax.ShapeDtypeStruct((16, kc), F32),
            jax.ShapeDtypeStruct((16, kc), F32),
        ),
        in_specs=[vmem] * 6 + [hbm] * 4 + [vmem] * 3,
        out_specs=(vmem,) * 5,
        scratch_shapes=scratch,
        compiler_params=pltpu.CompilerParams(
            collective_id=0, has_side_effects=True, vmem_limit_bytes=58 * 1024 * 1024
        ),
        cost_estimate=pl.CostEstimate(
            flops=2 * rows * width * hidden * 5, bytes_accessed=6 * width * hidden, transcendentals=0
        ),
    )(*args)
    return pl.pallas_call(
        hand_on,
        out_shape=tuple(jax.ShapeDtypeStruct(r.shape, r.dtype) for r in results),
        in_specs=[vmem] * len(results),
        out_specs=(vmem,) * len(results),
    )(*results)


def body(nz, hid, mix, og, gain, routes, rw, wg, wu, wd, a1, a2, att1, att2):
    ns = lax.axis_size("shard")
    width, kc = hid.shape[1], mix.shape[1]
    rg, ga, gs, af, sec = fused(
        nz,
        ns,
        hid,
        mix,
        og,
        gain.reshape(1, width),
        routes.T,
        rw.T,
        wg[0],
        wu[0],
        wd[0],
        a1[0].T,
        a2[0],
        att1.T,
        att2,
    )
    return rg, ga.T[None], gs[None], af.T, sec


def solution(mesh):
    nz = mesh.shape["dp"] // (2 * NX)
    in_specs = (
        P("dp", None),
        P("dp", "shard"),
        P("dp", None),
        P(),
        P("dp", None),
        P("dp", None),
        P("shard", None, "dp"),
        P("shard", None, "dp"),
        P("shard", "dp", None),
        P("shard", None, None),
        P("shard", None, "dp"),
        P("shard", None),
        P(None, "shard"),
    )
    out_specs = (
        P("dp", "shard"),
        P("shard", None, None),
        P("shard", None, "dp"),
        P("shard", None),
        P(None, "shard"),
    )
    return jax.shard_map(
        functools.partial(body, nz), mesh=mesh, in_specs=in_specs, out_specs=out_specs, check_vma=False
    )
```

```python
import functools

import jax
import jax.numpy as jnp
from jax import lax
from jax.experimental import pallas as pl
from jax.experimental.pallas import tpu as pltpu
from jax.sharding import PartitionSpec as P

CAP = 12
EPSILON = 1e-05
SCALE = 0.5
NX = 4
F32 = jnp.float32
BF16 = jnp.bfloat16
MESH = pl.DeviceIdType.MESH
NN = (((1,), (0,)), ((), ()))
NT = (((1,), (1,)), ((), ()))


GATHER = (
    ("I", 2), ("O", 2, 0), ("O", 0, 0), ("I", 3), ("O", 1, 0), ("I", 1), ("P1", 2, 0), ("P1", 2, 1),
    ("P1", 1, 0), ("P1", 3, 1), ("P2", 1, 0, 0), ("P1", 3, 0), ("I", 0), ("O", 3, 2), ("P1", 1, 1), ("F1", 2),
    ("F1", 3), ("F1", 1), ("P2", 2, 2, 1), ("P2", 2, 1, 1), ("P2", 2, 1, 0), ("O", 3, 1), ("P1", 0, 1),
    ("P2", 2, 3, 0), ("P2", 1, 1, 0), ("P2", 1, 0, 1), ("P1", 0, 0), ("P2", 2, 2, 0), ("P2", 2, 0, 1),
    ("O", 3, 3), ("P2", 2, 3, 1), ("O", 3, 0), ("P2", 1, 3, 1), ("P2", 1, 1, 1), ("P2", 1, 3, 0),
    ("P2", 2, 0, 0), ("F1", 0), ("P2", 1, 2, 0), ("P2", 1, 2, 1), ("P2", 3, 2, 0), ("D", 2), ("P2", 3, 1, 1),
    ("W", 2), ("P2", 0, 2, 0), ("P2", 0, 2, 1), ("P2", 3, 1, 0), ("P2", 3, 2, 1), ("P2", 0, 1, 0),
    ("P2", 0, 0, 1), ("P2", 0, 0, 0), ("P2", 0, 1, 1), ("D", 1), ("P2", 0, 3, 1), ("P2", 3, 0, 1),
    ("P2", 0, 3, 0), ("P2", 3, 0, 0), ("W", 1), ("T", 2), ("P2", 3, 3, 1), ("P2", 3, 3, 0), ("D", 0), ("T", 1),
    ("W", 0), ("D", 3), ("W", 3), ("T", 0), ("T", 3),
)
REDUCE = (
    ("P", 5), ("P", 4), ("P", 2), ("P", 3), ("A", 5), ("A", 4), ("A", 2), ("A", 3), ("B", 5, 1), ("B", 4, 0),
    ("S", 1), ("P", 6), ("B", 4, 1), ("B", 5, 0), ("P", 0), ("P", 7), ("B", 3, 0), ("B", 2, 1), ("A", 6),
    ("B", 2, 0), ("B", 3, 1), ("S", 2), ("A", 7), ("P", 1), ("A", 0), ("C", 2), ("B", 6, 0), ("B", 6, 1),
    ("A", 1), ("S", 3), ("B", 7, 1), ("B", 7, 0), ("C", 1), ("G", 6), ("B", 0, 0), ("B", 0, 1), ("B", 1, 0),
    ("B", 1, 1), ("D", 2), ("C", 3), ("G", 0), ("G", 4), ("C", 0), ("D", 1), ("G", 5), ("G", 1), ("G", 2),
    ("D", 3), ("D", 0), ("G", 7), ("G", 3),
)


def mm(a, b, dims=NN):
    return lax.dot_general(a, b, dims, preferred_element_type=F32)


def two_parts(value):
    high = value.astype(BF16)
    return high, (value - high.astype(F32)).astype(BF16)


def column(row, count):
    eye = lax.broadcasted_iota(jnp.int32, (count, count), 0) == lax.broadcasted_iota(
        jnp.int32, (count, count), 1
    )
    return jnp.sum(jnp.where(eye, jnp.broadcast_to(row, (count, count)), 0.0), axis=1, keepdims=True)


def row_of(col, count):
    eye = lax.broadcasted_iota(jnp.int32, (count, count), 0) == lax.broadcasted_iota(
        jnp.int32, (count, count), 1
    )
    return jnp.sum(jnp.where(eye, jnp.broadcast_to(col, (count, count)), 0.0), axis=0, keepdims=True)


def kernel(
    nz,
    ns,
    kc,
    hid_hbm,
    mix_hbm,
    og_hbm,
    gain_hbm,
    routes_hbm,
    rw_hbm,
    wg_hbm,
    wu_hbm,
    wd_hbm,
    a1_hbm,
    a2_hbm,
    att1_hbm,
    att2_hbm,
    rg_ref,
    ga_hbm,
    gs_ref,
    af_ref,
    as_ref,
    small,
    ga_ref,
    ga_sem,
    s_sem,
    wg,
    wu,
    wd,
    a1,
    rb,
    sb0,
    G,
    acc_g,
    acc_u,
    acc_d,
    acc_l,
    dg,
    du,
    bk,
    TB,
    TR,
    SB,
    XR1,
    XR2,
    ZB,
    ZR,
    EB,
    E,
    PB,
    PR,
    at_bufs,
    bk_bufs,
    rad_ref,
    w_sem,
    p0_s,
    p0_r,
    g_s,
    s1_r,
    s2_r,
    c_s,
    c_r,
    t_s,
    t_r,
    x_s,
    x1_r,
    x2_r,
    zz_s,
    zz_r,
    e_s,
    e_r,
    e_l,
    q_s,
    q_r,
    at_sems,
    bk_sems,
):
    hid_ref, mix_ref, og_ref, gain_ref, routes_ref, rw_ref, a2_ref, att1_ref, att2_ref = small
    small_hbm = (hid_hbm, mix_hbm, og_hbm, gain_hbm, routes_hbm, rw_hbm, a2_hbm, att1_hbm, att2_hbm)
    s_copies = [
        pltpu.make_async_copy(src, dst, s_sem.at[i]) for i, (src, dst) in enumerate(zip(small_hbm, small))
    ]
    for copy in s_copies:
        copy.start()

    nch = ns // 2
    nd = NX * nz * 2
    chips = NX * nz
    toks = hid_ref.shape[0]
    width = hid_ref.shape[1]
    hw = width // 2
    frame = chips * 32
    rows = chips * 24
    lanes = kc // 128
    d = lax.axis_index("dp")
    s = lax.axis_index("shard")
    core = lax.rem(d, 2)
    zh = lax.rem(d // 2, nz)
    xx = d // (2 * nz)
    q = xx * nz + zh
    other = 1 - core

    def dp_of(x_, z_, c_):
        return (x_ * nz + z_) * 2 + c_

    xp, xm, x2 = lax.rem(xx + 1, NX), lax.rem(xx + 3, NX), lax.rem(xx + 2, NX)
    dev_c = (dp_of(xx, zh, other), s)
    dev_xp = (dp_of(xp, zh, core), s)
    dev_xm = (dp_of(xm, zh, core), s)

    def zpeer(o):
        return lax.rem(zh + o, nz)

    def dev_z(o):
        return (dp_of(xx, zpeer(o), core), s)

    def rcopy(src, dst, ssem, rsem, dev):
        return pltpu.make_async_remote_copy(
            src_ref=src, dst_ref=dst, send_sem=ssem, recv_sem=rsem, device_id=dev, device_id_type=MESH
        )

    w_copies = [
        pltpu.make_async_copy(wg_hbm, wg, w_sem.at[0]),
        pltpu.make_async_copy(wu_hbm, wu, w_sem.at[1]),
    ] + [
        pltpu.make_async_copy(wd_hbm.at[:, pl.ds(i * kc, kc)], wd.at[i], w_sem.at[2 + i])
        for i in range(2 * nch)
    ] + [
        pltpu.make_async_copy(a1_hbm.at[:, pl.ds(i * kc, kc)], a1.at[i], w_sem.at[2 + 2 * nch + i])
        for i in range(2 * nch)
    ]

    barrier = pltpu.get_barrier_semaphore()

    def greet(dev):
        pl.semaphore_signal(barrier, inc=1, device_id=dev, device_id_type=MESH)

    group = [(dc, o) for dc in range(2) for o in range(NX)][1:]

    def dev_g(dc, o):
        return (dp_of(lax.rem(xx + o, NX), zh, other if dc else core), s)

    for dc, o in group:
        greet(dev_g(dc, o))
    for o in range(1, nz):
        greet(dev_z(o))

    def greet_shard(o, carry):
        there = lax.rem(s + o, ns)
        greet((d, there))
        greet((dp_of(xx, zh, other), there))
        return carry

    lax.fori_loop(1, ns, greet_shard, 0)

    for copy in w_copies:
        copy.start()
    for copy in s_copies:
        copy.wait()

    hid = hid_ref[...].astype(F32)
    radius = lax.rsqrt(jnp.mean(hid * hid, axis=1, keepdims=True) + EPSILON)
    rad_ref[...] = jnp.broadcast_to(radius, rad_ref.shape)
    normed = hid * radius * gain_ref[...]
    tok = jnp.concatenate([normed, og_ref[...].astype(F32)], axis=0).astype(BF16)

    r0 = column(routes_ref[0:1, :].astype(F32), toks)
    r1 = column(routes_ref[1:2, :].astype(F32), toks)
    w0 = column(rw_ref[0:1, :], toks)
    w1 = column(rw_ref[1:2, :], toks)
    lane = lax.broadcasted_iota(jnp.int32, (toks, 128), 1)
    lower = (
        lax.broadcasted_iota(jnp.int32, (toks, toks), 0) > lax.broadcasted_iota(jnp.int32, (toks, toks), 1)
    ).astype(F32).astype(BF16)
    lane_e = (lane // 16).astype(F32)
    named_all = jnp.where((r0 == lane_e) | (r1 == lane_e), 1.0, 0.0)
    slot_all = mm(lower, named_all.astype(BF16))
    place_f = lax.rem(lane, 16).astype(F32)
    choose_all = jnp.where(slot_all + (4 * core).astype(F32) == place_f, named_all, 0.0).astype(BF16)
    mine = jnp.broadcast_to(s.astype(F32), (toks, 128))
    hit0 = jnp.where(r0 == mine, 1.0, 0.0)
    hit1 = jnp.where(r1 == mine, 1.0, 0.0)
    named = hit0 + hit1
    weight = hit0 * w0 + hit1 * w1
    slot = mm(lower, named.astype(BF16)) + (CAP * core).astype(F32)
    row_x = jnp.where(lane < 24, lane, -1).astype(F32)
    row_y = jnp.where(
        (lane >= 24) & (lane < 32), lane - 8, jnp.where((lane >= 32) & (lane < 48), lane - 32, -1)
    ).astype(F32)
    hot_x = jnp.where(slot == row_x, named, 0.0)
    hot_y = jnp.where(slot == row_y, named, 0.0)
    blank = jnp.zeros((128 - 2 * toks, 128), F32)
    hot = jnp.concatenate([hot_x, hot_y, blank], axis=0).T
    scale = jnp.concatenate([hot_x, hot_y * weight, blank], axis=0).T
    hot = hot[0:48, 0:48].astype(BF16)
    scale = jnp.sum(scale[0:48, :], axis=1, keepdims=True)
    for j in range(2 * nch):
        part = mm(hot, tok[:, j * kc : (j + 1) * kc]) * scale
        sb0[j] = part.astype(BF16)

    pl.semaphore_wait(barrier, 2 * NX - 1 + nz - 1 + 2 * (ns - 1))

    swap = rcopy(sb0.at[pl.ds(other * nch, nch)], rb, p0_s, p0_r, dev_c)
    swap.start()

    mix_f = mix_ref[...].astype(F32)
    mix_rows = jnp.concatenate([jnp.zeros((96, kc), F32), mix_f, jnp.zeros((8, kc), F32)], axis=0)
    PB[8:24] = mm(att1_ref[...], mix_rows.astype(BF16), NT)

    class Sum:
        def __init__(self, bufs, sems):
            self.part, self.g_in, self.z_in, self.full = bufs
            self.send, self.g_r, self.z_r, self.b_r = sems
            self.n8 = self.part.shape[2]

        def where(self, t):
            return t // (4 * self.n8), (t // self.n8) % 4, t % self.n8

        def put(self, t, tile):
            self.part[self.where(t)] = tile

        def get(self, t):
            return self.full[self.where(t)]

        def g_copy(self, m):
            dc, o = group[m]
            src = self.part.at[other if dc else core, lax.rem(xx + o, NX)]
            return rcopy(src, self.g_in.at[m], self.send.at[m], self.g_r.at[m], dev_g(dc, o))

        def z_copy(self, o):
            ref = self.z_in.at[zh]
            return rcopy(ref, ref, self.send.at[6 + o], self.z_r.at[o - 1], dev_z(o))

        def b_copy(self, m):
            ref = self.full.at[core, xx]
            return rcopy(ref, ref, self.send.at[10 + m], self.b_r.at[m], dev_g(*group[m]))

        def step(self, n):
            if n == 0:
                for m in range(7):
                    self.g_copy(m).start()
            elif n == 1:
                total = self.part[core, xx]
                for m in range(7):
                    self.g_copy(m).wait_recv()
                    total = total + self.g_in[m]
                self.z_in[zh] = total
                for o in range(1, 4):
                    self.z_copy(o).start()
            elif n == 2:
                for o in range(1, 4):
                    self.z_copy(o).wait_recv()
                self.full[core, xx] = self.z_in[0] + self.z_in[1] + self.z_in[2] + self.z_in[3]
                for m in range(7):
                    self.b_copy(m).start()
            else:
                for m in range(7):
                    self.b_copy(m).wait_recv()

        def sent(self):
            for m in range(7):
                self.g_copy(m).wait_send()
                self.b_copy(m).wait_send()
            for o in range(1, 4):
                self.z_copy(o).wait_send()

    att_sum = Sum(at_bufs, at_sems)
    back_sum = Sum(bk_bufs, bk_sems)

    acc_g[...] = jnp.zeros_like(acc_g)
    acc_u[...] = jnp.zeros_like(acc_u)
    acc_d[...] = jnp.zeros_like(acc_d)
    acc_l[...] = jnp.zeros_like(acc_l)

    swap.wait_recv()

    zm, zp, z2 = lax.rem(zh + 3, nz), lax.rem(zh + 1, nz), lax.rem(zh + 2, nz)
    dev_zp, dev_zm = dev_z(1), dev_z(3)
    last = nch - 1
    xs_of, zs_of = (xx, xm, xp, x2), (zh, zm, zp, z2)

    def along(k, first):
        return (k != last) == first

    def ring(k, on_z, fixed, which, ssem, rsem):
        ch = core * nch + k
        if on_z:
            at, low_, high_, up, down = fixed * nz + zh, fixed * nz + zm, fixed * nz + zp, dev_zp, dev_zm
        else:
            at, low_, high_, up, down = xx * nz + fixed, xm * nz + fixed, xp * nz + fixed, dev_xp, dev_xm
        if which == 0:
            ref, dev = G.at[ch, at], up
        elif which == 1:
            ref, dev = G.at[ch, at], down
        elif which == 2:
            ref, dev = G.at[ch, low_, :, pl.ds(0, kc // 2)], up
        else:
            ref, dev = G.at[ch, high_, :, pl.ds(kc // 2, kc // 2)], down
        return rcopy(ref, ref, ssem, rsem, dev)

    def s1(k, which):
        on_z = along(k, True)
        return ring(k, on_z, xx if on_z else zh, which, g_s.at[k], s1_r.at[k, which])

    def s2(k, p, which):
        on_z = along(k, False)
        fixed = xs_of[p] if on_z else zs_of[p]
        return ring(k, on_z, fixed, which, g_s.at[k], s2_r.at[k, p, which])

    def c_copy(k, p=None):
        if p is None:
            ref, n = G.at[core * nch + k], 0
        else:
            ref, n = G.at[core * nch + k, pl.ds(xs_of[p] * nz, nz)], p
        return rcopy(ref, ref, c_s.at[k, n], c_r.at[k, n], dev_c)

    def piece(k):
        G[core * nch + k, q] = (sb0[core * nch + k].astype(F32) + rb[k].astype(F32)).astype(BF16)

    def s2_out(k, p):
        s2(k, p, 0).start()
        s2(k, p, 1).start()

    def s2_done(k):
        for p in range(4):
            s2(k, p, 2).wait_recv()
            s2(k, p, 3).wait_recv()
            if k == last:
                c_copy(k, p).start()
        if k != last:
            c_copy(k).start()

    def product(ch):
        xrows = G[ch, :, 0:32, :].reshape(frame, kc)
        yrows = G[ch, :, 16:48, :].reshape(frame, kc)
        at = pl.ds(pl.multiple_of(ch * kc, kc), kc)
        acc_g[...] += mm(xrows, wg[at, :])
        acc_u[...] += mm(xrows, wu[at, :])
        acc_l[:, 0:16] += mm(xrows, a1[ch], NT)
        acc_d[...] += mm(yrows, wd[ch], NT)

    def of_other(k):
        if k == last:
            for p in range(4):
                c_copy(k, p).wait_recv()
        else:
            c_copy(k).wait_recv()
        product(other * nch + k)

    placed = set()
    weights_here = False
    for name, k, *rest in GATHER:
        if name in ("I", "O") and k not in placed:
            placed.add(k)
            piece(k)
        if name == "I":
            s1(k, 0).start()
            s1(k, 1).start()
        elif name == "P1":
            which = rest[0]
            s1(k, which).wait_recv()
            s1(k, 2 + which).start()
            if k != last:
                s2_out(k, 1 + which)
        elif name == "F1":
            s1(k, 2).wait_recv()
            s1(k, 3).wait_recv()
            if k != last:
                s2_out(k, 3)
        elif name == "O":
            s2_out(k, rest[0])
        elif name == "P2":
            p, which = rest
            s2(k, p, which).wait_recv()
            s2(k, p, 2 + which).start()
        elif name == "D":
            s2_done(k)
        else:
            if not weights_here:
                weights_here = True
                for copy in w_copies:
                    copy.wait()
            if name == "W":
                product(core * nch + k)
            else:
                of_other(k)

    low = acc_l[...].astype(BF16)
    gate = acc_g[...] + SCALE * mm(low[:, 0:16], a2_ref[...])
    hidden = gate.shape[1]
    gate = gate.reshape(chips, 32, hidden)[:, 0:24, :]
    upper = acc_u[...].reshape(chips, 32, hidden)[:, 0:24, :]
    dact = acc_d[...].reshape(chips, 32, hidden)
    dact = jnp.concatenate([dact[:, 16:32, :], dact[:, 8:16, :]], axis=1)
    sig = 1.0 / (1.0 + jnp.exp(-gate))
    dgate = dact * upper * sig * (1.0 + gate * (1.0 - sig))
    dup = dact * gate * sig
    du[...] = dup.reshape(rows, hidden).astype(BF16)
    dgate_rows = dgate.reshape(rows, hidden).astype(BF16)
    dg[...] = dgate_rows
    bk[...] = (SCALE * mm(dgate_rows, a2_ref[...], NT)).astype(BF16)
    dgate_frame = (
        jnp.concatenate([dgate, jnp.zeros((chips, 8, hidden), F32)], axis=1)
        .reshape(frame, hidden)
        .astype(BF16)
    )
    low_t = acc_l[...].T[0:16, :].astype(BF16)
    gs_ref[...] = SCALE * mm(low_t, dgate_frame)
    back_t = SCALE * mm(a2_ref[...], dgate_frame, NT)
    f_lanes = frame // 128
    n_back = 2 * f_lanes
    for j in range(n_back):
        r, l = j // f_lanes, j % f_lanes
        back_sum.put(j, back_t[r * 8 : r * 8 + 8, l * 128 : (l + 1) * 128])

    back_sum.step(0)

    slab = nz * 24
    half_slab = slab // 2

    hc = kc // 2

    def term(half, j):
        ch = half * nch + j // 2
        at = pl.ds(pl.multiple_of(ch * kc + (j % 2) * hc, hc), hc)
        cols = slice((j % 2) * hc, (j % 2) * hc + hc)
        return mm(dg[...], wg[at, :], NT) + mm(du[...], wu[at, :], NT) + mm(bk[...], a1[ch, :, cols])

    def t_copy(k):
        return rcopy(TB.at[k], TR.at[k], t_s.at[k], t_r.at[k], dev_c)

    def x1_copy(k, which):
        if which == 0:
            return rcopy(
                SB.at[k, x2, pl.ds(0, half_slab)], XR1.at[k, 0], x_s.at[k], x1_r.at[k, 0], dev_xp
            )
        return rcopy(
            SB.at[k, x2, pl.ds(half_slab, half_slab)], XR1.at[k, 1], x_s.at[k], x1_r.at[k, 1], dev_xm
        )

    def x2_copy(k, which):
        if which == 0:
            return rcopy(SB.at[k, xp], XR2.at[k, 0], x_s.at[k], x2_r.at[k, 0], dev_xp)
        return rcopy(SB.at[k, xm], XR2.at[k, 1], x_s.at[k], x2_r.at[k, 1], dev_xm)

    def zz_copy(k, o):
        return rcopy(ZB.at[k, zpeer(o)], ZR.at[k, o - 1], zz_s.at[k], zz_r.at[k, o - 1], dev_z(o))

    def e_copy(k, c_):
        return rcopy(EB.at[k, c_], E.at[s], e_s.at[k, c_], e_r.at[s], (dp_of(xx, zh, c_), core * nch + k))

    def e_local(k, c_):
        return pltpu.make_async_copy(EB.at[k, c_], E.at[s], e_l)

    def e_self(k, c_):
        return (core * nch + k == s) & (core == c_)

    def send_term(j):
        TB[j] = term(other, j).astype(BF16)
        t_copy(j).start()

    def core_sum(j):
        own = term(core, j)
        t_copy(j).wait_recv()
        SB[j] = (own + TR[j].astype(F32)).astype(BF16).reshape(NX, slab, hc)
        x1_copy(j, 0).start()
        x1_copy(j, 1).start()

    def x_pass(j, which):
        there, at = ((xp, 0), (xm, half_slab))[which]
        x1_copy(j, which).wait_recv()
        SB[j, there, at : at + half_slab] = (
            SB[j, there, at : at + half_slab].astype(F32) + XR1[j, which].astype(F32)
        ).astype(BF16)
        x2_copy(j, which).start()

    def x_sum(j):
        x2_copy(j, 0).wait_recv()
        x2_copy(j, 1).wait_recv()
        return SB[j, xx].astype(F32) + XR2[j, 0].astype(F32) + XR2[j, 1].astype(F32)

    def z_send(k):
        left, right = x_sum(2 * k), x_sum(2 * k + 1)
        for z_ in range(nz):
            rows_ = slice(z_ * 24, z_ * 24 + 24)
            ZB[k, z_] = jnp.concatenate([left[rows_], right[rows_]], axis=0).astype(BF16)
        for o in range(1, nz):
            zz_copy(k, o).start()

    def z_sum(k):
        total = ZB[k, zh].astype(F32)
        for o in range(1, nz):
            zz_copy(k, o).wait_recv()
            total = total + ZR[k, o - 1].astype(F32)
        total = jnp.concatenate([total[0:24], total[24:48]], axis=1)
        EB[k, 0] = total[0:16].astype(BF16)
        EB[k, 1] = total[8:24].astype(BF16)
        for c_ in range(2):
            self_ = e_self(k, c_)

            @pl.when(self_)
            def _():
                e_local(k, c_).start()
                e_local(k, c_).wait()

            @pl.when(jnp.logical_not(self_))
            def _():
                e_copy(k, c_).start()

    def back_parts():
        back_full = jnp.concatenate(
            [
                jnp.concatenate([back_sum.get(r * f_lanes + l) for l in range(f_lanes)], axis=1)
                for r in range(2)
            ],
            axis=0,
        )
        high, rest = two_parts(back_full)
        both = jnp.concatenate([high, rest], axis=0)
        return both

    both, done = None, 0
    ga_copy = pltpu.make_async_copy(ga_ref, ga_hbm, ga_sem)
    for name, j, *rest in REDUCE:
        if name == "P":
            send_term(j)
        elif name == "A":
            core_sum(j)
        elif name == "B":
            x_pass(j, rest[0])
        elif name == "C":
            z_send(j)
        elif name == "D":
            z_sum(j)
        elif name == "S":
            back_sum.step(j)
        else:
            if both is None:
                both = back_parts()
            xrows = G[j, :, 0:32, :].reshape(frame, kc)
            pair = mm(both, xrows)
            ga_ref[:, j * kc : (j + 1) * kc] = pair[0:16] + pair[16:32]
            done += 1
            if done == 2 * nch:
                ga_copy.start()

    def e_wait(o, carry):
        there = lax.rem(s + o, ns)
        rcopy(E.at[there], E.at[there], e_s.at[0, 0], e_r.at[there], dev_c).wait_recv()
        return carry

    lax.fori_loop(1, ns, e_wait, 0)
    home = s // nch == core

    @pl.when(jnp.logical_not(home))
    def _():
        rcopy(E.at[s], E.at[s], e_s.at[0, 0], e_r.at[s], dev_c).wait_recv()

    at = pl.ds(pl.multiple_of(s * kc, kc), kc)
    grad = mm(choose_all[:, 0 : 16 * ns], E[...].reshape(16 * ns, kc))
    spread = gain_ref[:, at] * grad
    hid_cols = hid_ref[:, at]
    hid_f = hid_cols.astype(F32)
    rad = rad_ref[:, 0:1]
    base = og_ref[:, at].astype(F32) + rad * spread
    stat_part = jnp.sum(spread * hid_f, axis=1, keepdims=True)
    PB[0:8, 0:toks] = jnp.broadcast_to(row_of(stat_part, toks), (8, toks))
    high, rest = two_parts(base)
    gap = jnp.zeros((8, kc), F32)
    stack = jnp.concatenate(
        [high.astype(F32), gap, rest.astype(F32), gap, hid_f, gap, jnp.zeros((32, kc), F32)], axis=0
    )
    PB[8:24] = PB[8:24] + mm(att2_ref[...], stack.astype(BF16), NT)

    def q_copy(o):
        return rcopy(PB, PR.at[o - 1], q_s, q_r.at[o - 1], (d, lax.rem(s + o, ns)))

    for o in range(1, ns):
        q_copy(o).start()
    total = PB[...]
    for o in range(1, ns):
        q_copy(o).wait_recv()
        total = total + PR[o - 1]
    stat_row = total[0:1, 0:toks] / width
    factor = rad * rad * rad * column(stat_row, toks)
    rg = (base - hid_f * factor).astype(BF16)
    rg_ref[...] = rg
    factor_row = row_of(factor, toks)
    low_parts = total[8:24, :]
    back_low = (
        low_parts[:, 0:toks] + low_parts[:, 32 : 32 + toks] - low_parts[:, 64 : 64 + toks] * factor_row
    ).astype(BF16)
    mixed_low = low_parts[:, 96 : 96 + toks].astype(BF16)
    first = SCALE * mm(back_low, mix_ref[...])
    second = SCALE * mm(mixed_low, rg)
    for j in range(lanes):
        cols = slice(j * 128, (j + 1) * 128)
        att_sum.put(j, first[0:8, cols])
        att_sum.put(lanes + j, first[8:16, cols])
        att_sum.put(2 * lanes + j, second[0:8, cols])
        att_sum.put(3 * lanes + j, second[8:16, cols])
    att_sum.step(0)

    att_sum.step(1)
    att_sum.step(2)

    swap.wait_send()

    def drain(k, carry):
        sent = G.at[k, pl.ds(0, 15)]
        rcopy(sent, sent, g_s.at[k], g_s.at[k], dev_c).wait_send()
        sent = ZB.at[k, pl.ds(0, nz - 1)]
        rcopy(sent, sent, zz_s.at[k], zz_s.at[k], dev_c).wait_send()
        for j in range(2):
            t_copy(2 * k + j).wait_send()
            sent = TB.at[2 * k + j, pl.ds(0, 3 * slab)]
            rcopy(sent, sent, x_s.at[2 * k + j], x_s.at[2 * k + j], dev_c).wait_send()
        for c_ in range(2):

            @pl.when(jnp.logical_not(e_self(k, c_)))
            def _():
                e_copy(k, c_).wait_send()

        return carry

    lax.fori_loop(0, nch, drain, 0)
    for k in range(last):
        c_copy(k).wait_send()
    for p in range(4):
        c_copy(last, p).wait_send()
    rcopy(PR, PR, q_s, q_s, dev_c).wait_send()
    back_sum.sent()

    att_sum.step(3)
    for j in range(lanes):
        cols = slice(j * 128, (j + 1) * 128)
        af_ref[0:8, cols] = att_sum.get(j)
        af_ref[8:16, cols] = att_sum.get(lanes + j)
        as_ref[0:8, cols] = att_sum.get(2 * lanes + j)
        as_ref[8:16, cols] = att_sum.get(3 * lanes + j)
    att_sum.sent()
    ga_copy.wait()


def hand_on(*refs):
    count = len(refs) // 2
    for i in range(count):
        refs[count + i][...] = refs[i][...]


def fused(nz, ns, *args):
    hid, mix = args[0], args[1]
    width, kc = hid.shape[1], mix.shape[1]
    toks = hid.shape[0]
    hidden = args[6].shape[1]
    nch = ns // 2
    nd = NX * nz * 2
    chips = NX * nz
    rows, frame = chips * 24, chips * 32
    slab = nz * 24
    zo = max(nz - 1, 1)
    vm = pltpu.VMEM
    dma = pltpu.SemaphoreType.DMA
    sum_sems = (dma((17,)), dma((7,)), dma((3,)), dma((7,)))

    def tiles(count):
        n8 = count // 8
        return (
            vm((2, 4, n8, 8, 128), F32),
            vm((7, n8, 8, 128), F32),
            vm((4, n8, 8, 128), F32),
            vm((2, 4, n8, 8, 128), F32),
        )

    scratch = [
        tuple(vm(a.shape, a.dtype) for a in args[:6] + args[10:]),
        vm((16, width), F32),
        dma,
        dma((9,)),
        vm((width, hidden), BF16),
        vm((width, hidden), BF16),
        vm((2 * nch, hidden, kc), BF16),
        vm((2 * nch, 16, kc), BF16),
        vm((nch, 48, kc), BF16),
        vm((2 * nch, 48, kc), BF16),
        vm((2 * nch, chips, 48, kc), BF16),
        vm((frame, hidden), F32),
        vm((frame, hidden), F32),
        vm((frame, hidden), F32),
        vm((frame, 128), F32),
        vm((rows, hidden), BF16),
        vm((rows, hidden), BF16),
        vm((rows, 16), BF16),
        vm((2 * nch, rows, kc // 2), BF16),
        vm((2 * nch, rows, kc // 2), BF16),
        vm((2 * nch, NX, slab, kc // 2), BF16),
        vm((2 * nch, 2, slab // 2, kc // 2), BF16),
        vm((2 * nch, 2, slab, kc // 2), BF16),
        vm((nch, nz, 48, kc // 2), BF16),
        vm((nch, zo, 48, kc // 2), BF16),
        vm((nch, 2, 16, kc), BF16),
        vm((ns, 16, kc), BF16),
        vm((24, 128), F32),
        vm((ns - 1, 24, 128), F32),
        tiles(4 * kc // 128),
        tiles(2 * frame // 128),
        vm((toks, 128), F32),
        dma((2 + 4 * nch,)),
        dma,
        dma,
        dma((nch,)),
        dma((nch, 4)),
        dma((nch, 4, 4)),
        dma((nch, 4)),
        dma((nch, 4)),
        dma((2 * nch,)),
        dma((2 * nch,)),
        dma((2 * nch,)),
        dma((2 * nch, 2)),
        dma((2 * nch, 2)),
        dma((nch,)),
        dma((nch, zo)),
        dma((nch, 2)),
        dma((ns,)),
        dma,
        dma,
        dma((ns - 1,)),
        sum_sems,
        sum_sems,
    ]
    vmem = pl.BlockSpec(memory_space=pltpu.VMEM)
    hbm = pl.BlockSpec(memory_space=pl.ANY)
    results = pl.pallas_call(
        functools.partial(kernel, nz, ns, kc),
        out_shape=(
            jax.ShapeDtypeStruct((toks, kc), BF16),
            jax.ShapeDtypeStruct((16, width), F32),
            jax.ShapeDtypeStruct((16, hidden), F32),
            jax.ShapeDtypeStruct((16, kc), F32),
            jax.ShapeDtypeStruct((16, kc), F32),
        ),
        in_specs=[hbm] * len(args),
        out_specs=(vmem, hbm, vmem, vmem, vmem),
        scratch_shapes=scratch,
        compiler_params=pltpu.CompilerParams(
            collective_id=0, has_side_effects=True, vmem_limit_bytes=58 * 1024 * 1024
        ),
        cost_estimate=pl.CostEstimate(
            flops=2 * rows * width * hidden * 5, bytes_accessed=6 * width * hidden, transcendentals=0
        ),
    )(*args)
    return pl.pallas_call(
        hand_on,
        out_shape=tuple(jax.ShapeDtypeStruct(r.shape, r.dtype) for r in results),
        in_specs=[vmem] * len(results),
        out_specs=(vmem,) * len(results),
    )(*results)


def body(nz, hid, mix, og, gain, routes, rw, wg, wu, wd, a1, a2, att1, att2):
    ns = lax.axis_size("shard")
    width, kc = hid.shape[1], mix.shape[1]
    rg, ga, gs, af, sec = fused(
        nz,
        ns,
        hid,
        mix,
        og,
        gain.reshape(1, width),
        routes.T,
        rw.T,
        wg[0],
        wu[0],
        wd[0],
        a1[0].T,
        a2[0],
        att1.T,
        att2,
    )
    return rg, ga.T[None], gs[None], af.T, sec


def solution(mesh):
    nz = mesh.shape["dp"] // (2 * NX)
    in_specs = (
        P("dp", None),
        P("dp", "shard"),
        P("dp", None),
        P(),
        P("dp", None),
        P("dp", None),
        P("shard", None, "dp"),
        P("shard", None, "dp"),
        P("shard", "dp", None),
        P("shard", None, None),
        P("shard", None, "dp"),
        P("shard", None),
        P(None, "shard"),
    )
    out_specs = (
        P("dp", "shard"),
        P("shard", None, None),
        P("shard", None, "dp"),
        P("shard", None),
        P(None, "shard"),
    )
    return jax.shard_map(
        functools.partial(body, nz), mesh=mesh, in_specs=in_specs, out_specs=out_specs, check_vma=False
    )
```

```python
import functools

import jax
import jax.numpy as jnp
from jax import lax
from jax.experimental import pallas as pl
from jax.experimental.pallas import tpu as pltpu
from jax.sharding import PartitionSpec as P

CAP = 12
EPSILON = 1e-05
SCALE = 0.5
NX = 4
F32 = jnp.float32
BF16 = jnp.bfloat16
MESH = pl.DeviceIdType.MESH
NN = (((1,), (0,)), ((), ()))
NT = (((1,), (1,)), ((), ()))


GATHER = (
    ("I", 2), ("O", 2, 0), ("O", 0, 0), ("I", 3), ("O", 1, 0), ("I", 1), ("P1", 2, 0), ("P1", 2, 1),
    ("P1", 1, 0), ("P1", 3, 1), ("P2", 1, 0, 0), ("P1", 3, 0), ("I", 0), ("O", 3, 2), ("P1", 1, 1), ("F1", 2),
    ("F1", 3), ("F1", 1), ("P2", 2, 2, 1), ("P2", 2, 1, 1), ("P2", 2, 1, 0), ("O", 3, 1), ("P1", 0, 1),
    ("P2", 2, 3, 0), ("P2", 1, 1, 0), ("P2", 1, 0, 1), ("P1", 0, 0), ("P2", 2, 2, 0), ("P2", 2, 0, 1),
    ("O", 3, 3), ("P2", 2, 3, 1), ("O", 3, 0), ("P2", 1, 3, 1), ("P2", 1, 1, 1), ("P2", 1, 3, 0),
    ("P2", 2, 0, 0), ("F1", 0), ("P2", 1, 2, 0), ("P2", 1, 2, 1), ("P2", 3, 2, 0), ("D", 2), ("P2", 3, 1, 1),
    ("W", 2), ("P2", 0, 2, 0), ("P2", 0, 2, 1), ("P2", 3, 1, 0), ("P2", 3, 2, 1), ("P2", 0, 1, 0),
    ("P2", 0, 0, 1), ("P2", 0, 0, 0), ("P2", 0, 1, 1), ("D", 1), ("P2", 0, 3, 1), ("P2", 3, 0, 1),
    ("P2", 0, 3, 0), ("P2", 3, 0, 0), ("W", 1), ("T", 2), ("P2", 3, 3, 1), ("P2", 3, 3, 0), ("D", 0), ("T", 1),
    ("W", 0), ("D", 3), ("W", 3), ("T", 0), ("T", 3),
)
REDUCE = (
    ("P", 5), ("P", 4), ("P", 2), ("P", 3), ("A", 5), ("A", 4), ("A", 2), ("A", 3), ("B", 5, 1), ("B", 4, 0),
    ("S", 1), ("P", 6), ("B", 4, 1), ("B", 5, 0), ("P", 0), ("P", 7), ("B", 3, 0), ("B", 2, 1), ("A", 6),
    ("B", 2, 0), ("B", 3, 1), ("S", 2), ("A", 7), ("P", 1), ("A", 0), ("C", 2), ("B", 6, 0), ("B", 6, 1),
    ("A", 1), ("S", 3), ("B", 7, 1), ("B", 7, 0), ("C", 1), ("G", 6), ("B", 0, 0), ("B", 0, 1), ("B", 1, 0),
    ("B", 1, 1), ("D", 2), ("C", 3), ("G", 0), ("G", 4), ("C", 0), ("D", 1), ("G", 5), ("G", 1), ("G", 2),
    ("D", 3), ("D", 0), ("G", 7), ("G", 3),
)


def mm(a, b, dims=NN):
    return lax.dot_general(a, b, dims, preferred_element_type=F32)


def two_parts(value):
    high = value.astype(BF16)
    return high, (value - high.astype(F32)).astype(BF16)


def column(row, count):
    eye = lax.broadcasted_iota(jnp.int32, (count, count), 0) == lax.broadcasted_iota(
        jnp.int32, (count, count), 1
    )
    return jnp.sum(jnp.where(eye, jnp.broadcast_to(row, (count, count)), 0.0), axis=1, keepdims=True)


def row_of(col, count):
    eye = lax.broadcasted_iota(jnp.int32, (count, count), 0) == lax.broadcasted_iota(
        jnp.int32, (count, count), 1
    )
    return jnp.sum(jnp.where(eye, jnp.broadcast_to(col, (count, count)), 0.0), axis=0, keepdims=True)


def kernel(
    nz,
    ns,
    kc,
    hid_hbm,
    mix_hbm,
    og_hbm,
    gain_hbm,
    routes_hbm,
    rw_hbm,
    wg_hbm,
    wu_hbm,
    wd_hbm,
    a1_hbm,
    a2_hbm,
    att1_hbm,
    att2_hbm,
    rg_ref,
    ga_hbm,
    gs_ref,
    af_ref,
    as_ref,
    small,
    ga_ref,
    ga_sem,
    s_sem,
    wg,
    wu,
    wd,
    a1,
    rb,
    sb0,
    G,
    acc_g,
    acc_u,
    acc_d,
    acc_l,
    dg,
    du,
    bk,
    TB,
    TR,
    SB,
    XR1,
    XR2,
    ZB,
    ZR,
    EB,
    E,
    PB,
    PR,
    at_bufs,
    bk_bufs,
    rad_ref,
    w_sem,
    p0_s,
    p0_r,
    g_s,
    s1_r,
    s2_r,
    c_s,
    c_r,
    t_s,
    t_r,
    x_s,
    x1_r,
    x2_r,
    zz_s,
    zz_r,
    e_s,
    e_r,
    e_l,
    q_s,
    q_r,
    at_sems,
    bk_sems,
):
    hid_ref, mix_ref, og_ref, gain_ref, routes_ref, rw_ref, a2_ref, att1_ref, att2_ref = small
    small_hbm = (hid_hbm, mix_hbm, og_hbm, gain_hbm, routes_hbm, rw_hbm, a2_hbm, att1_hbm, att2_hbm)
    s_copies = [
        pltpu.make_async_copy(src, dst, s_sem.at[i]) for i, (src, dst) in enumerate(zip(small_hbm, small))
    ]
    nch = ns // 2
    nd = NX * nz * 2
    chips = NX * nz
    toks = hid_ref.shape[0]
    width = hid_ref.shape[1]
    hw = width // 2
    frame = chips * 32
    rows = chips * 24
    lanes = kc // 128
    d = lax.axis_index("dp")
    s = lax.axis_index("shard")
    core = lax.rem(d, 2)
    zh = lax.rem(d // 2, nz)
    xx = d // (2 * nz)
    q = xx * nz + zh
    other = 1 - core

    def dp_of(x_, z_, c_):
        return (x_ * nz + z_) * 2 + c_

    xp, xm, x2 = lax.rem(xx + 1, NX), lax.rem(xx + 3, NX), lax.rem(xx + 2, NX)
    dev_c = (dp_of(xx, zh, other), s)
    dev_xp = (dp_of(xp, zh, core), s)
    dev_xm = (dp_of(xm, zh, core), s)

    def zpeer(o):
        return lax.rem(zh + o, nz)

    def dev_z(o):
        return (dp_of(xx, zpeer(o), core), s)

    def rcopy(src, dst, ssem, rsem, dev):
        return pltpu.make_async_remote_copy(
            src_ref=src, dst_ref=dst, send_sem=ssem, recv_sem=rsem, device_id=dev, device_id_type=MESH
        )

    w_copies = [
        pltpu.make_async_copy(wg_hbm, wg, w_sem.at[0]),
        pltpu.make_async_copy(wu_hbm, wu, w_sem.at[1]),
    ] + [
        pltpu.make_async_copy(wd_hbm.at[:, pl.ds(i * kc, kc)], wd.at[i], w_sem.at[2 + i])
        for i in range(2 * nch)
    ] + [
        pltpu.make_async_copy(a1_hbm.at[:, pl.ds(i * kc, kc)], a1.at[i], w_sem.at[2 + 2 * nch + i])
        for i in range(2 * nch)
    ]

    barrier = pltpu.get_barrier_semaphore()

    def greet(dev):
        pl.semaphore_signal(barrier, inc=1, device_id=dev, device_id_type=MESH)

    group = [(dc, o) for dc in range(2) for o in range(NX)][1:]

    def dev_g(dc, o):
        return (dp_of(lax.rem(xx + o, NX), zh, other if dc else core), s)

    for dc, o in group:
        greet(dev_g(dc, o))
    for o in range(1, nz):
        greet(dev_z(o))

    def greet_shard(o, carry):
        there = lax.rem(s + o, ns)
        greet((d, there))
        greet((dp_of(xx, zh, other), there))
        return carry

    lax.fori_loop(1, ns, greet_shard, 0)

    for copy in s_copies:
        copy.start()
    for copy in w_copies:
        copy.start()
    for copy in s_copies:
        copy.wait()

    hid = hid_ref[...].astype(F32)
    radius = lax.rsqrt(jnp.mean(hid * hid, axis=1, keepdims=True) + EPSILON)
    rad_ref[...] = jnp.broadcast_to(radius, rad_ref.shape)
    normed = hid * radius * gain_ref[...]
    tok = jnp.concatenate([normed, og_ref[...].astype(F32)], axis=0).astype(BF16)

    r0 = column(routes_ref[0:1, :].astype(F32), toks)
    r1 = column(routes_ref[1:2, :].astype(F32), toks)
    w0 = column(rw_ref[0:1, :], toks)
    w1 = column(rw_ref[1:2, :], toks)
    lane = lax.broadcasted_iota(jnp.int32, (toks, 128), 1)
    lower = (
        lax.broadcasted_iota(jnp.int32, (toks, toks), 0) > lax.broadcasted_iota(jnp.int32, (toks, toks), 1)
    ).astype(F32).astype(BF16)
    lane_e = (lane // 16).astype(F32)
    named_all = jnp.where((r0 == lane_e) | (r1 == lane_e), 1.0, 0.0)
    slot_all = mm(lower, named_all.astype(BF16))
    place_f = lax.rem(lane, 16).astype(F32)
    choose_all = jnp.where(slot_all + (4 * core).astype(F32) == place_f, named_all, 0.0).astype(BF16)
    mine = jnp.broadcast_to(s.astype(F32), (toks, 128))
    hit0 = jnp.where(r0 == mine, 1.0, 0.0)
    hit1 = jnp.where(r1 == mine, 1.0, 0.0)
    named = hit0 + hit1
    weight = hit0 * w0 + hit1 * w1
    slot = mm(lower, named.astype(BF16)) + (CAP * core).astype(F32)
    row_x = jnp.where(lane < 24, lane, -1).astype(F32)
    row_y = jnp.where(
        (lane >= 24) & (lane < 32), lane - 8, jnp.where((lane >= 32) & (lane < 48), lane - 32, -1)
    ).astype(F32)
    hot_x = jnp.where(slot == row_x, named, 0.0)
    hot_y = jnp.where(slot == row_y, named, 0.0)
    blank = jnp.zeros((128 - 2 * toks, 128), F32)
    hot = jnp.concatenate([hot_x, hot_y, blank], axis=0).T
    scale = jnp.concatenate([hot_x, hot_y * weight, blank], axis=0).T
    hot = hot[0:48, 0:48].astype(BF16)
    scale = jnp.sum(scale[0:48, :], axis=1, keepdims=True)
    for j in range(2 * nch):
        part = mm(hot, tok[:, j * kc : (j + 1) * kc]) * scale
        sb0[j] = part.astype(BF16)

    pl.semaphore_wait(barrier, 2 * NX - 1 + nz - 1 + 2 * (ns - 1))

    swap = rcopy(sb0.at[pl.ds(other * nch, nch)], rb, p0_s, p0_r, dev_c)
    swap.start()

    mix_f = mix_ref[...].astype(F32)
    mix_rows = jnp.concatenate([jnp.zeros((96, kc), F32), mix_f, jnp.zeros((8, kc), F32)], axis=0)
    PB[8:24] = mm(att1_ref[...], mix_rows.astype(BF16), NT)

    class Sum:
        def __init__(self, bufs, sems):
            self.part, self.g_in, self.z_in, self.full = bufs
            self.send, self.g_r, self.z_r, self.b_r = sems
            self.n8 = self.part.shape[2]

        def where(self, t):
            return t // (4 * self.n8), (t // self.n8) % 4, t % self.n8

        def put(self, t, tile):
            self.part[self.where(t)] = tile

        def get(self, t):
            return self.full[self.where(t)]

        def g_copy(self, m):
            dc, o = group[m]
            src = self.part.at[other if dc else core, lax.rem(xx + o, NX)]
            return rcopy(src, self.g_in.at[m], self.send.at[m], self.g_r.at[m], dev_g(dc, o))

        def z_copy(self, o):
            ref = self.z_in.at[zh]
            return rcopy(ref, ref, self.send.at[6 + o], self.z_r.at[o - 1], dev_z(o))

        def b_copy(self, m):
            ref = self.full.at[core, xx]
            return rcopy(ref, ref, self.send.at[10 + m], self.b_r.at[m], dev_g(*group[m]))

        def step(self, n):
            if n == 0:
                for m in range(7):
                    self.g_copy(m).start()
            elif n == 1:
                total = self.part[core, xx]
                for m in range(7):
                    self.g_copy(m).wait_recv()
                    total = total + self.g_in[m]
                self.z_in[zh] = total
                for o in range(1, 4):
                    self.z_copy(o).start()
            elif n == 2:
                for o in range(1, 4):
                    self.z_copy(o).wait_recv()
                self.full[core, xx] = self.z_in[0] + self.z_in[1] + self.z_in[2] + self.z_in[3]
                for m in range(7):
                    self.b_copy(m).start()
            else:
                for m in range(7):
                    self.b_copy(m).wait_recv()

        def sent(self):
            for m in range(7):
                self.g_copy(m).wait_send()
                self.b_copy(m).wait_send()
            for o in range(1, 4):
                self.z_copy(o).wait_send()

    att_sum = Sum(at_bufs, at_sems)
    back_sum = Sum(bk_bufs, bk_sems)

    acc_g[...] = jnp.zeros_like(acc_g)
    acc_u[...] = jnp.zeros_like(acc_u)
    acc_d[...] = jnp.zeros_like(acc_d)
    acc_l[...] = jnp.zeros_like(acc_l)

    swap.wait_recv()

    zm, zp, z2 = lax.rem(zh + 3, nz), lax.rem(zh + 1, nz), lax.rem(zh + 2, nz)
    dev_zp, dev_zm = dev_z(1), dev_z(3)
    last = nch - 1
    xs_of, zs_of = (xx, xm, xp, x2), (zh, zm, zp, z2)

    def along(k, first):
        return (k != last) == first

    def ring(k, on_z, fixed, which, ssem, rsem):
        ch = core * nch + k
        if on_z:
            at, low_, high_, up, down = fixed * nz + zh, fixed * nz + zm, fixed * nz + zp, dev_zp, dev_zm
        else:
            at, low_, high_, up, down = xx * nz + fixed, xm * nz + fixed, xp * nz + fixed, dev_xp, dev_xm
        if which == 0:
            ref, dev = G.at[ch, at], up
        elif which == 1:
            ref, dev = G.at[ch, at], down
        elif which == 2:
            ref, dev = G.at[ch, low_, :, pl.ds(0, kc // 2)], up
        else:
            ref, dev = G.at[ch, high_, :, pl.ds(kc // 2, kc // 2)], down
        return rcopy(ref, ref, ssem, rsem, dev)

    def s1(k, which):
        on_z = along(k, True)
        return ring(k, on_z, xx if on_z else zh, which, g_s.at[k], s1_r.at[k, which])

    def s2(k, p, which):
        on_z = along(k, False)
        fixed = xs_of[p] if on_z else zs_of[p]
        return ring(k, on_z, fixed, which, g_s.at[k], s2_r.at[k, p, which])

    def c_copy(k, p=None):
        if p is None:
            ref, n = G.at[core * nch + k], 0
        else:
            ref, n = G.at[core * nch + k, pl.ds(xs_of[p] * nz, nz)], p
        return rcopy(ref, ref, c_s.at[k, n], c_r.at[k, n], dev_c)

    def piece(k):
        G[core * nch + k, q] = (sb0[core * nch + k].astype(F32) + rb[k].astype(F32)).astype(BF16)

    def s2_out(k, p):
        s2(k, p, 0).start()
        s2(k, p, 1).start()

    def s2_done(k):
        for p in range(4):
            s2(k, p, 2).wait_recv()
            s2(k, p, 3).wait_recv()
            if k == last:
                c_copy(k, p).start()
        if k != last:
            c_copy(k).start()

    def product(ch):
        xrows = G[ch, :, 0:32, :].reshape(frame, kc)
        yrows = G[ch, :, 16:48, :].reshape(frame, kc)
        at = pl.ds(pl.multiple_of(ch * kc, kc), kc)
        acc_g[...] += mm(xrows, wg[at, :])
        acc_u[...] += mm(xrows, wu[at, :])
        acc_l[:, 0:16] += mm(xrows, a1[ch], NT)
        acc_d[...] += mm(yrows, wd[ch], NT)

    def of_other(k):
        if k == last:
            for p in range(4):
                c_copy(k, p).wait_recv()
        else:
            c_copy(k).wait_recv()
        product(other * nch + k)

    placed = set()
    weights_here = False
    for name, k, *rest in GATHER:
        if name in ("I", "O") and k not in placed:
            placed.add(k)
            piece(k)
        if name == "I":
            s1(k, 0).start()
            s1(k, 1).start()
        elif name == "P1":
            which = rest[0]
            s1(k, which).wait_recv()
            s1(k, 2 + which).start()
            if k != last:
                s2_out(k, 1 + which)
        elif name == "F1":
            s1(k, 2).wait_recv()
            s1(k, 3).wait_recv()
            if k != last:
                s2_out(k, 3)
        elif name == "O":
            s2_out(k, rest[0])
        elif name == "P2":
            p, which = rest
            s2(k, p, which).wait_recv()
            s2(k, p, 2 + which).start()
        elif name == "D":
            s2_done(k)
        else:
            if not weights_here:
                weights_here = True
                for copy in w_copies:
                    copy.wait()
            if name == "W":
                product(core * nch + k)
            else:
                of_other(k)

    low = acc_l[...].astype(BF16)
    gate = acc_g[...] + SCALE * mm(low[:, 0:16], a2_ref[...])
    hidden = gate.shape[1]
    gate = gate.reshape(chips, 32, hidden)[:, 0:24, :]
    upper = acc_u[...].reshape(chips, 32, hidden)[:, 0:24, :]
    dact = acc_d[...].reshape(chips, 32, hidden)
    dact = jnp.concatenate([dact[:, 16:32, :], dact[:, 8:16, :]], axis=1)
    sig = 1.0 / (1.0 + jnp.exp(-gate))
    dgate = dact * upper * sig * (1.0 + gate * (1.0 - sig))
    dup = dact * gate * sig
    du[...] = dup.reshape(rows, hidden).astype(BF16)
    dgate_rows = dgate.reshape(rows, hidden).astype(BF16)
    dg[...] = dgate_rows
    bk[...] = (SCALE * mm(dgate_rows, a2_ref[...], NT)).astype(BF16)
    dgate_frame = (
        jnp.concatenate([dgate, jnp.zeros((chips, 8, hidden), F32)], axis=1)
        .reshape(frame, hidden)
        .astype(BF16)
    )
    low_t = acc_l[...].T[0:16, :].astype(BF16)
    gs_ref[...] = SCALE * mm(low_t, dgate_frame)
    back_t = SCALE * mm(a2_ref[...], dgate_frame, NT)
    f_lanes = frame // 128
    n_back = 2 * f_lanes
    for j in range(n_back):
        r, l = j // f_lanes, j % f_lanes
        back_sum.put(j, back_t[r * 8 : r * 8 + 8, l * 128 : (l + 1) * 128])

    back_sum.step(0)

    slab = nz * 24
    half_slab = slab // 2

    hc = kc // 2

    def term(half, j):
        ch = half * nch + j // 2
        at = pl.ds(pl.multiple_of(ch * kc + (j % 2) * hc, hc), hc)
        cols = slice((j % 2) * hc, (j % 2) * hc + hc)
        return mm(dg[...], wg[at, :], NT) + mm(du[...], wu[at, :], NT) + mm(bk[...], a1[ch, :, cols])

    def t_copy(k):
        return rcopy(TB.at[k], TR.at[k], t_s.at[k], t_r.at[k], dev_c)

    def x1_copy(k, which):
        if which == 0:
            return rcopy(
                SB.at[k, x2, pl.ds(0, half_slab)], XR1.at[k, 0], x_s.at[k], x1_r.at[k, 0], dev_xp
            )
        return rcopy(
            SB.at[k, x2, pl.ds(half_slab, half_slab)], XR1.at[k, 1], x_s.at[k], x1_r.at[k, 1], dev_xm
        )

    def x2_copy(k, which):
        if which == 0:
            return rcopy(SB.at[k, xp], XR2.at[k, 0], x_s.at[k], x2_r.at[k, 0], dev_xp)
        return rcopy(SB.at[k, xm], XR2.at[k, 1], x_s.at[k], x2_r.at[k, 1], dev_xm)

    def zz_copy(k, o):
        return rcopy(ZB.at[k, zpeer(o)], ZR.at[k, o - 1], zz_s.at[k], zz_r.at[k, o - 1], dev_z(o))

    def e_copy(k, c_):
        return rcopy(EB.at[k, c_], E.at[s], e_s.at[k, c_], e_r.at[s], (dp_of(xx, zh, c_), core * nch + k))

    def e_local(k, c_):
        return pltpu.make_async_copy(EB.at[k, c_], E.at[s], e_l)

    def e_self(k, c_):
        return (core * nch + k == s) & (core == c_)

    def send_term(j):
        TB[j] = term(other, j).astype(BF16)
        t_copy(j).start()

    def core_sum(j):
        own = term(core, j)
        t_copy(j).wait_recv()
        SB[j] = (own + TR[j].astype(F32)).astype(BF16).reshape(NX, slab, hc)
        x1_copy(j, 0).start()
        x1_copy(j, 1).start()

    def x_pass(j, which):
        there, at = ((xp, 0), (xm, half_slab))[which]
        x1_copy(j, which).wait_recv()
        SB[j, there, at : at + half_slab] = (
            SB[j, there, at : at + half_slab].astype(F32) + XR1[j, which].astype(F32)
        ).astype(BF16)
        x2_copy(j, which).start()

    def x_sum(j):
        x2_copy(j, 0).wait_recv()
        x2_copy(j, 1).wait_recv()
        return SB[j, xx].astype(F32) + XR2[j, 0].astype(F32) + XR2[j, 1].astype(F32)

    def z_send(k):
        left, right = x_sum(2 * k), x_sum(2 * k + 1)
        for z_ in range(nz):
            rows_ = slice(z_ * 24, z_ * 24 + 24)
            ZB[k, z_] = jnp.concatenate([left[rows_], right[rows_]], axis=0).astype(BF16)
        for o in range(1, nz):
            zz_copy(k, o).start()

    def z_sum(k):
        total = ZB[k, zh].astype(F32)
        for o in range(1, nz):
            zz_copy(k, o).wait_recv()
            total = total + ZR[k, o - 1].astype(F32)
        total = jnp.concatenate([total[0:24], total[24:48]], axis=1)
        EB[k, 0] = total[0:16].astype(BF16)
        EB[k, 1] = total[8:24].astype(BF16)
        for c_ in range(2):
            self_ = e_self(k, c_)

            @pl.when(self_)
            def _():
                e_local(k, c_).start()
                e_local(k, c_).wait()

            @pl.when(jnp.logical_not(self_))
            def _():
                e_copy(k, c_).start()

    def back_parts():
        back_full = jnp.concatenate(
            [
                jnp.concatenate([back_sum.get(r * f_lanes + l) for l in range(f_lanes)], axis=1)
                for r in range(2)
            ],
            axis=0,
        )
        high, rest = two_parts(back_full)
        both = jnp.concatenate([high, rest], axis=0)
        return both

    both, done = None, 0
    ga_copy = pltpu.make_async_copy(ga_ref, ga_hbm, ga_sem)
    for name, j, *rest in REDUCE:
        if name == "P":
            send_term(j)
        elif name == "A":
            core_sum(j)
        elif name == "B":
            x_pass(j, rest[0])
        elif name == "C":
            z_send(j)
        elif name == "D":
            z_sum(j)
        elif name == "S":
            back_sum.step(j)
        else:
            if both is None:
                both = back_parts()
            xrows = G[j, :, 0:32, :].reshape(frame, kc)
            pair = mm(both, xrows)
            ga_ref[:, j * kc : (j + 1) * kc] = pair[0:16] + pair[16:32]
            done += 1
            if done == 2 * nch:
                ga_copy.start()

    at = pl.ds(pl.multiple_of(s * kc, kc), kc)
    hid_f = hid_ref[:, at].astype(F32)
    og_f = og_ref[:, at].astype(F32)
    gain_cols = gain_ref[:, at]
    rad = rad_ref[:, 0:1]
    def e_wait(o, carry):
        there = lax.rem(s + o, ns)
        rcopy(E.at[there], E.at[there], e_s.at[0, 0], e_r.at[there], dev_c).wait_recv()
        return carry

    lax.fori_loop(1, ns, e_wait, 0)
    home = s // nch == core

    @pl.when(jnp.logical_not(home))
    def _():
        rcopy(E.at[s], E.at[s], e_s.at[0, 0], e_r.at[s], dev_c).wait_recv()

    grad = mm(choose_all[:, 0 : 16 * ns], E[...].reshape(16 * ns, kc))
    spread = gain_cols * grad
    base = og_f + rad * spread
    stat_part = jnp.sum(spread * hid_f, axis=1, keepdims=True)
    PB[0:8, 0:toks] = jnp.broadcast_to(row_of(stat_part, toks), (8, toks))
    high, rest = two_parts(base)
    gap = jnp.zeros((8, kc), F32)
    stack = jnp.concatenate(
        [high.astype(F32), gap, rest.astype(F32), gap, hid_f, gap, jnp.zeros((32, kc), F32)], axis=0
    )
    PB[8:24] = PB[8:24] + mm(att2_ref[...], stack.astype(BF16), NT)

    def q_copy(o):
        return rcopy(PB, PR.at[o - 1], q_s, q_r.at[o - 1], (d, lax.rem(s + o, ns)))

    for o in range(1, ns):
        q_copy(o).start()
    total = PB[...]
    for o in range(1, ns):
        q_copy(o).wait_recv()
        total = total + PR[o - 1]
    stat_row = total[0:1, 0:toks] / width
    factor = rad * rad * rad * column(stat_row, toks)
    rg = (base - hid_f * factor).astype(BF16)
    rg_ref[...] = rg
    factor_row = row_of(factor, toks)
    low_parts = total[8:24, :]
    back_low = (
        low_parts[:, 0:toks] + low_parts[:, 32 : 32 + toks] - low_parts[:, 64 : 64 + toks] * factor_row
    ).astype(BF16)
    mixed_low = low_parts[:, 96 : 96 + toks].astype(BF16)
    first = SCALE * mm(back_low, mix_ref[...])
    second = SCALE * mm(mixed_low, rg)
    for j in range(lanes):
        cols = slice(j * 128, (j + 1) * 128)
        att_sum.put(j, first[0:8, cols])
        att_sum.put(lanes + j, first[8:16, cols])
        att_sum.put(2 * lanes + j, second[0:8, cols])
        att_sum.put(3 * lanes + j, second[8:16, cols])
    att_sum.step(0)

    att_sum.step(1)
    att_sum.step(2)

    swap.wait_send()

    def drain(k, carry):
        sent = G.at[k, pl.ds(0, 15)]
        rcopy(sent, sent, g_s.at[k], g_s.at[k], dev_c).wait_send()
        sent = ZB.at[k, pl.ds(0, nz - 1)]
        rcopy(sent, sent, zz_s.at[k], zz_s.at[k], dev_c).wait_send()
        for j in range(2):
            t_copy(2 * k + j).wait_send()
            sent = TB.at[2 * k + j, pl.ds(0, 3 * slab)]
            rcopy(sent, sent, x_s.at[2 * k + j], x_s.at[2 * k + j], dev_c).wait_send()
        for c_ in range(2):

            @pl.when(jnp.logical_not(e_self(k, c_)))
            def _():
                e_copy(k, c_).wait_send()

        return carry

    lax.fori_loop(0, nch, drain, 0)
    for k in range(last):
        c_copy(k).wait_send()
    for p in range(4):
        c_copy(last, p).wait_send()
    rcopy(PR, PR, q_s, q_s, dev_c).wait_send()
    back_sum.sent()

    att_sum.step(3)
    for j in range(lanes):
        cols = slice(j * 128, (j + 1) * 128)
        af_ref[0:8, cols] = att_sum.get(j)
        af_ref[8:16, cols] = att_sum.get(lanes + j)
        as_ref[0:8, cols] = att_sum.get(2 * lanes + j)
        as_ref[8:16, cols] = att_sum.get(3 * lanes + j)
    att_sum.sent()
    ga_copy.wait()


def hand_on(*refs):
    count = len(refs) // 2
    for i in range(count):
        refs[count + i][...] = refs[i][...]


def fused(nz, ns, *args):
    hid, mix = args[0], args[1]
    width, kc = hid.shape[1], mix.shape[1]
    toks = hid.shape[0]
    hidden = args[6].shape[1]
    nch = ns // 2
    nd = NX * nz * 2
    chips = NX * nz
    rows, frame = chips * 24, chips * 32
    slab = nz * 24
    zo = max(nz - 1, 1)
    vm = pltpu.VMEM
    dma = pltpu.SemaphoreType.DMA
    sum_sems = (dma((17,)), dma((7,)), dma((3,)), dma((7,)))

    def tiles(count):
        n8 = count // 8
        return (
            vm((2, 4, n8, 8, 128), F32),
            vm((7, n8, 8, 128), F32),
            vm((4, n8, 8, 128), F32),
            vm((2, 4, n8, 8, 128), F32),
        )

    scratch = [
        tuple(vm(a.shape, a.dtype) for a in args[:6] + args[10:]),
        vm((16, width), F32),
        dma,
        dma((9,)),
        vm((width, hidden), BF16),
        vm((width, hidden), BF16),
        vm((2 * nch, hidden, kc), BF16),
        vm((2 * nch, 16, kc), BF16),
        vm((nch, 48, kc), BF16),
        vm((2 * nch, 48, kc), BF16),
        vm((2 * nch, chips, 48, kc), BF16),
        vm((frame, hidden), F32),
        vm((frame, hidden), F32),
        vm((frame, hidden), F32),
        vm((frame, 128), F32),
        vm((rows, hidden), BF16),
        vm((rows, hidden), BF16),
        vm((rows, 16), BF16),
        vm((2 * nch, rows, kc // 2), BF16),
        vm((2 * nch, rows, kc // 2), BF16),
        vm((2 * nch, NX, slab, kc // 2), BF16),
        vm((2 * nch, 2, slab // 2, kc // 2), BF16),
        vm((2 * nch, 2, slab, kc // 2), BF16),
        vm((nch, nz, 48, kc // 2), BF16),
        vm((nch, zo, 48, kc // 2), BF16),
        vm((nch, 2, 16, kc), BF16),
        vm((ns, 16, kc), BF16),
        vm((24, 128), F32),
        vm((ns - 1, 24, 128), F32),
        tiles(4 * kc // 128),
        tiles(2 * frame // 128),
        vm((toks, 128), F32),
        dma((2 + 4 * nch,)),
        dma,
        dma,
        dma((nch,)),
        dma((nch, 4)),
        dma((nch, 4, 4)),
        dma((nch, 4)),
        dma((nch, 4)),
        dma((2 * nch,)),
        dma((2 * nch,)),
        dma((2 * nch,)),
        dma((2 * nch, 2)),
        dma((2 * nch, 2)),
        dma((nch,)),
        dma((nch, zo)),
        dma((nch, 2)),
        dma((ns,)),
        dma,
        dma,
        dma((ns - 1,)),
        sum_sems,
        sum_sems,
    ]
    vmem = pl.BlockSpec(memory_space=pltpu.VMEM)
    hbm = pl.BlockSpec(memory_space=pl.ANY)
    results = pl.pallas_call(
        functools.partial(kernel, nz, ns, kc),
        out_shape=(
            jax.ShapeDtypeStruct((toks, kc), BF16),
            jax.ShapeDtypeStruct((16, width), F32),
            jax.ShapeDtypeStruct((16, hidden), F32),
            jax.ShapeDtypeStruct((16, kc), F32),
            jax.ShapeDtypeStruct((16, kc), F32),
        ),
        in_specs=[hbm] * len(args),
        out_specs=(vmem, hbm, vmem, vmem, vmem),
        scratch_shapes=scratch,
        compiler_params=pltpu.CompilerParams(
            collective_id=0, has_side_effects=True, vmem_limit_bytes=58 * 1024 * 1024
        ),
        cost_estimate=pl.CostEstimate(
            flops=2 * rows * width * hidden * 5, bytes_accessed=6 * width * hidden, transcendentals=0
        ),
    )(*args)
    return pl.pallas_call(
        hand_on,
        out_shape=tuple(jax.ShapeDtypeStruct(r.shape, r.dtype) for r in results),
        in_specs=[vmem] * len(results),
        out_specs=(vmem,) * len(results),
    )(*results)


def body(nz, hid, mix, og, gain, routes, rw, wg, wu, wd, a1, a2, att1, att2):
    ns = lax.axis_size("shard")
    width, kc = hid.shape[1], mix.shape[1]
    rg, ga, gs, af, sec = fused(
        nz,
        ns,
        hid,
        mix,
        og,
        gain.reshape(1, width),
        routes.T,
        rw.T,
        wg[0],
        wu[0],
        wd[0],
        a1[0].T,
        a2[0],
        att1.T,
        att2,
    )
    return rg, ga.T[None], gs[None], af.T, sec


def solution(mesh):
    nz = mesh.shape["dp"] // (2 * NX)
    in_specs = (
        P("dp", None),
        P("dp", "shard"),
        P("dp", None),
        P(),
        P("dp", None),
        P("dp", None),
        P("shard", None, "dp"),
        P("shard", None, "dp"),
        P("shard", "dp", None),
        P("shard", None, None),
        P("shard", None, "dp"),
        P("shard", None),
        P(None, "shard"),
    )
    out_specs = (
        P("dp", "shard"),
        P("shard", None, None),
        P("shard", None, "dp"),
        P("shard", None),
        P(None, "shard"),
    )
    return jax.shard_map(
        functools.partial(body, nz), mesh=mesh, in_specs=in_specs, out_specs=out_specs, check_vma=False
    )
```
